32 devices in a mesh: groups: 2 (over x), tensor: 8 (over z, y), replica: 2 (over core).
Axes of the slice: x: 2, y: 2, z: 4, core: 2. Of those that a mesh axis runs over, the one named last changes fastest.
Arguments:
- tokens: bfloat16 [2048, 8192], P(('groups', 'replica'), 'tensor'), parts along dimension 0, may hold values from -6 to 6
- context: bfloat16 [2048, 8192], P(('groups', 'replica'), 'tensor'), parts along dimension 0, may hold values from -6 to 6
- query_weight: bfloat16 [8192, 8192], P(None, 'tensor'), may hold values from -0.0625 to 0.0625
- output_weight: bfloat16 [8192, 8192], P('tensor'), may hold values from -0.09375 to 0.09375
- store_aq: bfloat16 [64, 64, 8192], P(('groups', 'replica'), None, 'tensor'), parts along dimension 0, may hold values from -0.0625 to 0.0625
- store_bq: bfloat16 [64, 64, 8192], P(('groups', 'replica'), None, 'tensor'), parts along dimension 0, may hold values from -0.75 to 0.75
- store_ao: bfloat16 [64, 64, 8192], P(('groups', 'replica'), None, 'tensor'), parts along dimension 0, may hold values from -0.0625 to 0.0625
- store_bo: bfloat16 [64, 64, 8192], P(('groups', 'replica'), None, 'tensor'), parts along dimension 0, may hold values from -0.75 to 0.75
- adapter_of: int32 [8], P('groups'), parts along dimension 0, may hold values from 0 to 31
- location: int32 [64], P('groups'), parts along dimension 0, may hold values from 0 to 31, each once
- token_count: int32 [8], P('groups'), parts along dimension 0, may hold values from 1 to 256, 768 in all
Outputs:
- queries: bfloat16 [2048, 8192], P(('groups', 'replica'), 'tensor'), parts along dimension 0
- attended: bfloat16 [2048, 8192], P(('groups', 'replica'), 'tensor'), parts along dimension 0
The draws below stay inside these ranges and needn't reach their ends.
There are 2 independent parts, one for each index of `groups`. The reference program is written for one: setup_inputs(seed, part) draws one part's arguments, and reference() takes and returns one part's arrays. A program takes and returns all parts, laid end to end along the dimension named above; an argument that names none is the same for every part. Nothing has to cross between parts.
Inputs may be any that keep to these rules, and one draw needn't show every extreme that they name: `location`: a permutation; store slots i * 16 to (i + 1) * 16 - 1 lie on index i of replica. `token_count`: one request reaches 256 in every draw; they sum to 768.
All inputs are finite; a program needn't handle non-finite values.
Results may differ from the reference program's by a relative error of at most 0.0029.
Values may be sent and summed in bfloat16 or wider, within the bound.
No kernel may reach another device: no remote copies, remote signals or barrier semaphores. Data moves between devices by JAX's collectives and lax.ppermute only.
A program may use at most 192 MiB of HBM per device.

```python
import math
import jax
import jax.numpy as jnp
import numpy as np

D = 8192
RANK = 64
REQUEST_LENGTH = 256
REQS = 4
TOKENS = 1024
NADP = 32


def set_ends(result, key, smallest, top_value):
    shape = result.shape
    index_at = [jax.random.randint(jax.random.fold_in(key, axis), (), 0, shape[axis]) for axis in range(len(shape))]
    result = result.at[tuple(index_at)].set(smallest)
    longest = shape.index(max(shape))
    index_at[longest] = (index_at[longest] + 1) % shape[longest]
    return result.at[tuple(index_at)].set(top_value)


def raised(values, rng, source, target, blocks, factor):
    def block_of(axis_at):
        return (jnp.arange(values.shape[axis_at]) // (values.shape[axis_at] // blocks)).reshape((-1,) + (1,) * (values.ndim - 1 - axis_at))

    one_side = jax.random.permutation(rng, blocks)[block_of(target)]
    second = (block_of(target) + blocks // 2) % blocks
    return jnp.where((block_of(source) == one_side) | (block_of(source) == second), factor * values, values)


def block_scale(key, shape, shards, least, top_value):
    factor_of = 1.0
    for position, blocks in shards:
        draws = jax.random.uniform(jax.random.fold_in(jax.random.fold_in(key, 6), position), (blocks,), jnp.float32, least / len(shards), top_value / len(shards))
        factor_of = factor_of * jnp.repeat(jnp.exp(draws), shape[position] // blocks).reshape((-1,) + (1,) * (len(shape) - 1 - position))
    return factor_of


def rank_table(number_of, slope):
    loads = [(1 << 20) // math.isqrt(rank ** slope) + 1 for rank in range(1, number_of + 1)]
    spread = 1 + sum(loads) // (1 << 30)
    return np.cumsum(np.array([max(1, weight // spread) for weight in loads]))


def ranked(rng, shape, amount, slope):
    listing = rank_table(amount, slope)
    pick = jax.random.randint(jax.random.fold_in(rng, 1), shape, 0, int(listing[amount - 1]))
    rank = jnp.searchsorted(jnp.asarray(listing, jnp.int32), pick, side="right")
    return jax.random.permutation(jax.random.fold_in(rng, 2), amount)[rank].astype(jnp.int32)


def split_up(number_of, total, reach, skew):
    portions = [(1 << 20) // math.isqrt(grade ** skew) + 1 for grade in range(2, number_of + 1)]
    surplus, given = total - reach - (number_of - 1), [1] * (number_of - 1)
    while surplus > 0:
        free = [i for i in range(number_of - 1) if given[i] < reach]
        mass, left = sum([portions[i] for i in free]), surplus
        for i in free:
            extra = min(reach - given[i], max(1, left * portions[i] // mass), surplus)
            given[i] = given[i] + extra
            surplus = surplus - extra
    return np.array([reach] + given)


def ragged_sizes(rng, amount, total, most, skew):
    if amount == 2:
        one = jax.random.randint(rng, (), max(1, total - most), min(most, total - 1) + 1)
        return jnp.stack([one, total - one])
    lengths = jnp.asarray(split_up(amount, total, most, skew), jnp.int32)
    couples = (amount - 1) // 2
    donor, receiver = lengths[1:1 + 2 * couples:2], lengths[2:2 + 2 * couples:2]
    slack = jnp.minimum(donor - 1, most - receiver)
    shifted = jax.random.randint(jax.random.fold_in(rng, 1), (couples,), 0, 1 << 20) % (slack + 1)
    lengths = lengths.at[1:1 + 2 * couples:2].set(donor - shifted).at[2:2 + 2 * couples:2].set(receiver + shifted)
    return lengths[jax.random.permutation(jax.random.fold_in(rng, 2), amount)]


def scatter_about(stream_key, dims, width, most, cuts=(), held_as=jnp.bfloat16):
    drawn = width * jax.random.normal(stream_key, dims, jnp.float32)
    if cuts:
        drawn = drawn * block_scale(stream_key, dims, cuts, -0.22, 0.18)
    return jnp.clip(drawn, -most, most).astype(held_as)


def gaussian_with(own_key, shape, deviation, bound, pieces, heavy, held_as=jnp.bfloat16):
    array = deviation * jax.random.normal(own_key, shape, jnp.float32)
    if pieces:
        array = array * block_scale(own_key, shape, pieces, -0.22, 0.18)
    return jnp.clip(raised(array, jax.random.fold_in(own_key, 3), *heavy), -bound, bound).astype(held_as)


def setup_inputs(seed: int = 0, part: int = 0) -> dict:
    key_list = jax.random.split(jax.random.key(seed), 12)
    part_splits = jax.random.split(jax.random.fold_in(key_list[11], part), 12)
    tokens = scatter_about(part_splits[0], (TOKENS, D), 1.0, 6.0, ((0, 2), (1, 8)))
    context = scatter_about(part_splits[1], (TOKENS, D), 1.0, 6.0, ((0, 2), (1, 8)))
    query_weight = scatter_about(key_list[2], (D, D), D ** -0.5, 0.0625, ((1, 8),))
    output_weight = gaussian_with(key_list[3], (D, D), D ** -0.5, 0.09375, ((0, 8),), (0, 1, 8, 2.0))
    store_aq = scatter_about(part_splits[4], (NADP, RANK, D), D ** -0.5, 0.0625, ((0, 2), (2, 8)))
    store_bq = scatter_about(part_splits[5], (NADP, RANK, D), RANK ** -0.5, 0.75, ((0, 2), (2, 8)))
    store_ao = scatter_about(part_splits[6], (NADP, RANK, D), D ** -0.5, 0.0625, ((0, 2), (2, 8)))
    store_bo = scatter_about(part_splits[7], (NADP, RANK, D), RANK ** -0.5, 0.75, ((0, 2), (2, 8)))
    adapter_of = set_ends(ranked(part_splits[8], (REQS,), NADP, 2), jax.random.fold_in(part_splits[8], 3), 0, NADP - 1).astype(jnp.int32)
    location = jax.random.permutation(part_splits[9], NADP).astype(jnp.int32)
    token_count = ragged_sizes(part_splits[10], REQS, 3 * REQS * REQUEST_LENGTH // 4, REQUEST_LENGTH, 2).astype(jnp.int32)
    return {"tokens": tokens, "context": context, "query_weight": query_weight, "output_weight": output_weight, "store_aq": store_aq, "store_bq": store_bq, "store_ao": store_ao, "store_bo": store_bo, "adapter_of": adapter_of, "location": location, "token_count": token_count}


adapter_scale = 0.5


def reference(tokens, context, query_weight, output_weight, store_aq, store_bq, store_ao, store_bo, adapter_of, location, token_count):
    slot = jnp.take(location, adapter_of, axis=0).astype(jnp.int32)
    query_base_rows = jnp.dot(tokens, query_weight, preferred_element_type=jnp.float32).reshape(REQS, REQUEST_LENGTH, D)
    output_base_rows = jnp.dot(context, output_weight, preferred_element_type=jnp.float32).reshape(REQS, REQUEST_LENGTH, D)
    rows_q = tokens.reshape(REQS, REQUEST_LENGTH, D).astype(jnp.float32)
    rows_o = context.reshape(REQS, REQUEST_LENGTH, D).astype(jnp.float32)
    down_aq = jnp.take(store_aq, slot, axis=0).astype(jnp.float32)
    down_ao = jnp.take(store_ao, slot, axis=0).astype(jnp.float32)
    up_bq = jnp.take(store_bq, slot, axis=0).astype(jnp.float32)
    up_bo = jnp.take(store_bo, slot, axis=0).astype(jnp.float32)
    down_q = jnp.einsum("rld,rkd->rlk", rows_q, down_aq).astype(jnp.bfloat16)
    down_o = jnp.einsum("rld,rkd->rlk", rows_o, down_ao).astype(jnp.bfloat16)
    query_adapter_delta = jnp.einsum("rlk,rke->rle", down_q.astype(jnp.float32), up_bq)
    output_adapter_delta = jnp.einsum("rlk,rke->rle", down_o.astype(jnp.float32), up_bo)
    active_rows = jnp.arange(REQUEST_LENGTH, dtype=jnp.int32)[None, :, None] < token_count[:, None, None]
    queries = jnp.where(active_rows, query_base_rows + adapter_scale * query_adapter_delta, jnp.float32(0.0)).astype(jnp.bfloat16)
    attended = jnp.where(active_rows, output_base_rows + adapter_scale * output_adapter_delta, jnp.float32(0.0)).astype(jnp.bfloat16)
    return queries.reshape(TOKENS, D), attended.reshape(TOKENS, D)
```

```python
import jax
import jax.numpy as jnp
from jax import lax
from jax.sharding import PartitionSpec as P

REQUEST_LENGTH = 256
SPLIT = 256

adapter_scale = 0.5

SUM_SCALE = 8.0
DOWN_SCALE = 16.0

BF16 = jnp.bfloat16
F16 = jnp.float16
F32 = jnp.float32


def z_pairs(*pairs):
    return [(2 * a + y, 2 * b + y) for a, b in pairs for y in range(2)]


INNER = z_pairs((1, 2), (2, 1))
OUTWARD = z_pairs((2, 3), (1, 0))
INWARD = z_pairs((0, 1), (3, 2))
SIDES = z_pairs((0, 1), (1, 0), (2, 3), (3, 2))
Y_SWAP = [(t, t ^ 1) for t in range(8)]
FAR = z_pairs((0, 2), (2, 0), (1, 3), (3, 1))


def send(value, pairs):
    return lax.ppermute(value, "tensor", pairs)


def other_replica(value):
    return lax.ppermute(value, "replica", [(0, 1), (1, 0)])


def dot(a, b):
    return jnp.dot(a, b, preferred_element_type=F32)


def pick(z, table):
    return jnp.asarray(table, jnp.int32)[z]


def by_z(z, table):
    out = jnp.int32(table[0])
    for i in range(1, 4):
        out = jnp.where(z == i, jnp.int32(table[i]), out)
    return out


def plan(token_count, replica, rows, packed):
    per = rows // REQUEST_LENGTH
    mine = lax.dynamic_slice_in_dim(token_count, replica * per, per)
    theirs = lax.dynamic_slice_in_dim(token_count, (1 - replica) * per, per)
    n_mine, n_theirs = jnp.sum(mine), jnp.sum(theirs)
    spare = rows - packed
    first = packed - spare
    length = jnp.arange(rows, dtype=jnp.int32) % REQUEST_LENGTH
    request = jnp.arange(rows, dtype=jnp.int32) // REQUEST_LENGTH
    start = jnp.cumsum(mine) - mine
    start_of = jnp.zeros((rows,), jnp.int32)
    count_of = jnp.zeros((rows,), jnp.int32)
    for i in range(per):
        start_of = jnp.where(request == i, start[i], start_of)
        count_of = jnp.where(request == i, mine[i], count_of)
    position = jnp.where(length < count_of, start_of + length, -1)
    here = jnp.where(position < packed, position, -1)
    there = jnp.where(position >= packed, position - packed + n_theirs - first, -1)
    pack_here = (jnp.arange(packed, dtype=jnp.int32)[:, None] == here[None, :]).astype(BF16)
    pack_there = (jnp.arange(spare, dtype=jnp.int32)[:, None] == there[None, :]).astype(BF16)
    unpack = jnp.concatenate([pack_here, pack_there], axis=0).T
    slot = jnp.arange(packed, dtype=jnp.int32)
    own = slot < n_mine
    seat = jnp.where(own, slot, packed + slot - n_mine)
    bounds_mine, bounds_theirs = jnp.cumsum(mine), jnp.cumsum(theirs)
    index = jnp.zeros((packed,), jnp.int32)
    for i in range(per - 1):
        index = index + (seat >= jnp.where(own, bounds_mine[i], bounds_theirs[i])).astype(jnp.int32)
    request_of = jnp.where(own, replica, 1 - replica) * per + index
    return pack_here, pack_there, unpack, request_of


def fetch(stores, slots, replica):
    held = stores[0].shape[0]
    picked = []
    for table in stores:
        for i in range(slots.shape[0]):
            local = slots[i] - replica * held
            mine = (local >= 0) & (local < held)
            block = lax.dynamic_index_in_dim(table, jnp.clip(local, 0, held - 1), 0, keepdims=False)
            picked.append(jnp.where(mine, block, jnp.zeros_like(block)))
    blocks = jnp.stack(picked)
    blocks = blocks + other_replica(blocks)
    rank, width = blocks.shape[1:]
    return blocks.reshape(len(stores), slots.shape[0] * rank, width)


def fits(mesh):
    return mesh.shape["tensor"] == 8


def gather_z(x, z):
    edge = (z == 0) | (z == 3)
    near_in, near_out = send(x, INNER), send(x, OUTWARD)
    one = jnp.where(edge, near_out, near_in)
    two = send(jnp.where(edge, x, one), SIDES)
    mid = send(two, INNER)
    out = send(mid, OUTWARD)
    three = jnp.where(edge, out, mid)
    return [x, one, two, three]


ONE = (1, 2, 1, 2)
TWO = (2, 0, 3, 1)
THREE = (3, 3, 0, 0)


def narrow(value):
    return (value * SUM_SCALE).astype(F16)


def widen(value):
    return value.astype(F32) * (1.0 / SUM_SCALE)


def scatter_z(part, z):
    edge = (z == 0) | (z == 3)
    p_far = part(0)
    r1 = send(narrow(p_far), INWARD)
    r2 = send(narrow(p_far + widen(r1)), INNER)
    r3 = send(narrow(part(1) + widen(r2)), SIDES)
    p_near = part(2)
    r4a = send(narrow(p_near), INWARD)
    r4b = send(narrow(p_near + widen(r3)), INNER)
    return part(3) + jnp.where(edge, widen(r3), widen(r4a) + widen(r4b))


def exchange(
    tokens, context, query_weight, output_weight, sum_down, z, y
):
    packed, width = tokens.shape
    a_tok, b_tok = tokens[:SPLIT], tokens[SPLIT:]
    a_ctx, b_ctx = context[:SPLIT], context[SPLIT:]
    owners = (THREE, TWO, ONE, (0, 1, 2, 3))
    shards = ((0, 1, 2, 3), ONE, TWO, THREE)

    def out_block(first, count):
        return lax.dynamic_slice_in_dim(output_weight, first * width, count * width, axis=1)

    def in_block(first, count):
        return lax.dynamic_slice_in_dim(query_weight, first * width, count * width, axis=0)

    b_pair = send(b_tok, Y_SWAP)
    a_from_y = [
        send(narrow(dot(a_ctx, out_block(2 * by_z(z, o) + 1 - y, 1))), Y_SWAP) for o in owners
    ]
    a_line = gather_z(a_tok, z)
    b_sum = scatter_z(lambda i: dot(b_ctx, out_block(2 * by_z(z, owners[i]), 2)), z)
    a_sum = scatter_z(
        lambda i: dot(a_ctx, out_block(2 * by_z(z, owners[i]) + y, 1)) + widen(a_from_y[i]), z
    )
    b_both = jnp.concatenate(
        [jnp.where(y == 0, b_tok, b_pair), jnp.where(y == 0, b_pair, b_tok)], axis=1
    )
    b_line = gather_z(b_both, z)
    a_cross = [send(v, Y_SWAP) for v in a_line]
    b_mine = lax.dynamic_slice_in_dim(b_sum, y * width, width, axis=1)
    b_theirs = lax.dynamic_slice_in_dim(b_sum, (1 - y) * width, width, axis=1)
    b_sum = b_mine + widen(send(narrow(b_theirs), Y_SWAP))

    a_q = jnp.zeros((SPLIT, query_weight.shape[1]), F32)
    b_q = jnp.zeros((packed - SPLIT, query_weight.shape[1]), F32)
    for i in range(4):
        at = by_z(z, shards[i])
        a_q = a_q + dot(a_line[i], in_block(2 * at + y, 1)) + dot(a_cross[i], in_block(2 * at + 1 - y, 1))
        b_q = b_q + dot(b_line[i], in_block(2 * at, 2))
    return jnp.concatenate([a_q, b_q]), jnp.concatenate([a_sum, b_sum])


def sum_over_tensor(part):
    total = part
    for pairs in (Y_SWAP, SIDES, FAR):
        moved = send((total * DOWN_SCALE).astype(F16), pairs)
        total = (total * DOWN_SCALE).astype(F16).astype(F32) * (1.0 / DOWN_SCALE)
        total = total + moved.astype(F32) * (1.0 / DOWN_SCALE)
    return total


def make(mesh):
    grid = fits(mesh)

    def local(
        tokens, context, query_weight, output_weight,
        store_aq, store_bq, store_ao, store_bo,
        adapter_of, location, token_count,
    ):
        rows, width = tokens.shape
        rank = store_aq.shape[1]
        packed = rows * 3 // 4
        spare = rows - packed
        first = packed - spare
        replica = lax.axis_index("replica")
        at = lax.axis_index("tensor")
        z, y = at // 2, at % 2
        pack_here, pack_there, unpack, request_of = plan(token_count, replica, rows, packed)
        slots = jnp.take(location, adapter_of, axis=0)

        pack = jnp.concatenate([pack_here, pack_there])
        both = dot(pack, jnp.concatenate([tokens, context], axis=1)).astype(BF16)
        moved = other_replica(both[packed:])
        both = jnp.concatenate([both[:first], both[first:packed] + moved])
        tok, ctx = both[:, :width], both[:, width:]

        down_aq, up_bq, down_ao, up_bo = fetch((store_aq, store_bq, store_ao, store_bo), slots, replica)
        chosen = (
            request_of[:, None] == jnp.arange(slots.shape[0] * rank, dtype=jnp.int32)[None, :] // rank
        )

        def fold(wide):
            return jnp.where(chosen, wide, 0.0).reshape(packed, slots.shape[0], rank).sum(1)

        part_q = fold(lax.dot_general(tok, down_aq, (((1,), (1,)), ((), ())), preferred_element_type=F32))
        part_o = fold(lax.dot_general(ctx, down_ao, (((1,), (1,)), ((), ())), preferred_element_type=F32))
        parts = jnp.concatenate([part_q, part_o], axis=1)

        if grid:
            low = sum_over_tensor(parts)
            base_q, base_o = exchange(tok, ctx, query_weight, output_weight, low, z, y)
        else:
            low = lax.psum(parts, "tensor")
            base_q = dot(lax.all_gather(tok, "tensor", axis=1, tiled=True), query_weight)
            base_o = lax.psum_scatter(dot(ctx, output_weight), "tensor", scatter_dimension=1, tiled=True)
        low = low.astype(BF16)

        def up(narrow_rows, blocks):
            spread = jnp.where(chosen, jnp.tile(narrow_rows, (1, slots.shape[0])), jnp.zeros((), BF16))
            return dot(spread, blocks)

        queries = (base_q + adapter_scale * up(low[:, :rank], up_bq)).astype(BF16)
        attended = (base_o + adapter_scale * up(low[:, rank:], up_bo)).astype(BF16)
        result = jnp.concatenate([queries, attended], axis=1)
        back = other_replica(result[first:])
        out = dot(unpack, jnp.concatenate([result, back])).astype(BF16)
        return out[:, :width], out[:, width:]

    return local


def solution(mesh):
    return jax.shard_map(
        make(mesh),
        mesh=mesh,
        in_specs=(
            P(("groups", "replica"), "tensor"),
            P(("groups", "replica"), "tensor"),
            P(None, "tensor"),
            P("tensor", None),
            P(("groups", "replica"), None, "tensor"),
            P(("groups", "replica"), None, "tensor"),
            P(("groups", "replica"), None, "tensor"),
            P(("groups", "replica"), None, "tensor"),
            P("groups"),
            P("groups"),
            P("groups"),
        ),
        out_specs=(P(("groups", "replica"), "tensor"), P(("groups", "replica"), "tensor")),
        check_vma=False,
    )
```

```python
import functools

import jax
import jax.numpy as jnp
from jax import lax
from jax.experimental import pallas as pl
from jax.experimental.pallas import tpu as pltpu
from jax.sharding import PartitionSpec as P

REQUEST_LENGTH = 256

adapter_scale = 0.5

SUM_SCALE = 8.0
DOWN_SCALE = 16.0

BF16 = jnp.bfloat16
F16 = jnp.float16
F32 = jnp.float32
I32 = jnp.int32

VMEM_LIMIT = 48 * 1024 * 1024


def z_pairs(*pairs):
    return [(2 * a + y, 2 * b + y) for a, b in pairs for y in range(2)]


INNER = z_pairs((1, 2), (2, 1))
OUTWARD = z_pairs((2, 3), (1, 0))
INWARD = z_pairs((0, 1), (3, 2))
SIDES = z_pairs((0, 1), (1, 0), (2, 3), (3, 2))
Y_SWAP = [(t, t ^ 1) for t in range(8)]
FAR = z_pairs((0, 2), (2, 0), (1, 3), (3, 1))

OWN = (0, 1, 2, 3)
ONE = (1, 2, 1, 2)
TWO = (2, 0, 3, 1)
THREE = (3, 3, 0, 0)


def send(value, pairs):
    return lax.ppermute(value, "tensor", pairs)


def other_replica(value):
    return lax.ppermute(value, "replica", [(0, 1), (1, 0)])


def dot(a, b):
    return jnp.dot(a, b, preferred_element_type=F32)


def dot_t(a, b):
    return lax.dot_general(a, b, (((1,), (1,)), ((), ())), preferred_element_type=F32)


def by_z(z, table):
    out = I32(table[0])
    for i in range(1, 4):
        out = jnp.where(z == i, I32(table[i]), out)
    return out


def whole(shape):
    return pl.BlockSpec(shape, lambda *_: (0,) * len(shape))


def params(n=1):
    return pltpu.CompilerParams(
        dimension_semantics=("arbitrary",) * n, vmem_limit_bytes=VMEM_LIMIT
    )


def iota(shape, dim):
    return lax.broadcasted_iota(I32, shape, dim)


def pack_kernel(counts, x_ref, a_ref, b_ref, spare_ref):
    rows = x_ref.shape[0]
    first, spare = a_ref.shape[0], spare_ref.shape[0]
    packed = first + b_ref.shape[0]
    c_a, n_mine = counts[0], counts[0] + counts[1]
    n_theirs = counts[2] + counts[3]

    def take(position, live):
        home = jnp.where(position < c_a, position, REQUEST_LENGTH + position - c_a)
        hot = iota((position.shape[0], rows), 1) == jnp.where(live, home, -1)
        return dot(hot.astype(F32).astype(BF16), x_ref[...]).astype(BF16)

    slot = iota((packed, 1), 0)
    here = take(slot, slot < n_mine)
    a_ref[...] = here[:first]
    b_ref[...] = here[first:]
    seat = iota((spare, 1), 0) + first - n_theirs
    spare_ref[...] = take(packed + seat, seat >= 0)


def pack(counts, x, packed):
    rows, width = x.shape
    spare = rows - packed
    first = packed - spare
    shapes = [(first, width), (packed - first, width), (spare, width)]
    return pl.pallas_call(
        pack_kernel,
        grid_spec=pltpu.PrefetchScalarGridSpec(
            num_scalar_prefetch=1,
            grid=(1,),
            in_specs=[whole(x.shape)],
            out_specs=[whole(s) for s in shapes],
        ),
        out_shape=[jax.ShapeDtypeStruct(s, BF16) for s in shapes],
        compiler_params=params(),
        name="pack_rows",
    )(counts, x)


def unpack_kernel(counts, qa, qb, qc, oa, ob, oc, q_ref, o_ref):
    rows = q_ref.shape[0]
    first = qa.shape[0]
    packed = first + qb.shape[0]
    c_a, c_b = counts[0], counts[1]
    n_theirs = counts[2] + counts[3]
    row = iota((rows, 1), 0)
    late = row >= REQUEST_LENGTH
    offset = jnp.where(late, row - REQUEST_LENGTH, row)
    position = offset + jnp.where(late, c_a, 0)
    target = jnp.where(position < packed, position, position + n_theirs - first)
    target = jnp.where(offset < jnp.where(late, c_b, c_a), target, -1)
    hot = (iota((rows, rows), 1) == target).astype(F32).astype(BF16)
    for a, b, c, out in ((qa, qb, qc, q_ref), (oa, ob, oc, o_ref)):
        out[...] = (
            dot(hot[:, :first], a[...]) + dot(hot[:, first:packed], b[...]) + dot(hot[:, packed:], c[...])
        ).astype(BF16)


def unpack(counts, rows, parts):
    width = parts[0].shape[1]
    shape = (rows, width)
    return pl.pallas_call(
        unpack_kernel,
        grid_spec=pltpu.PrefetchScalarGridSpec(
            num_scalar_prefetch=1,
            grid=(1,),
            in_specs=[whole(p.shape) for p in parts],
            out_specs=[whole(shape)] * 2,
        ),
        out_shape=[jax.ShapeDtypeStruct(shape, BF16)] * 2,
        compiler_params=params(),
        name="unpack_rows",
    )(counts, *parts)


def request_of(counts, slot, packed):
    c_a, n_mine, d_a = counts[0], counts[0] + counts[1], counts[2]
    replica = counts[4]
    own = slot < n_mine
    seat = jnp.where(own, slot, packed + slot - n_mine)
    mine = 2 * replica + (seat >= c_a).astype(I32)
    theirs = 2 * (1 - replica) + (seat >= d_a).astype(I32)
    return jnp.where(own, mine, theirs)


def fetch_kernel(adapter_of, location, replica, *refs):
    stores, out = refs[:4], refs[4]
    held = pl.num_programs(0)
    del held
    i = pl.program_id(0)
    slot = location[adapter_of[i]] - replica[0] * replica[1]
    mine = (slot >= 0) & (slot < replica[1])
    for k, table in enumerate(stores):
        block = table[0]
        out[k] = jnp.where(mine, block, jnp.zeros_like(block))


def fetch(stores, adapter_of, location, replica):
    held, rank, width = stores[0].shape
    requests = adapter_of.shape[0]

    def at(i, adapter_of, location, replica):
        slot = location[adapter_of[i]] - replica[0] * held
        return jnp.clip(slot, 0, held - 1), 0, 0

    return pl.pallas_call(
        fetch_kernel,
        grid_spec=pltpu.PrefetchScalarGridSpec(
            num_scalar_prefetch=3,
            grid=(requests,),
            in_specs=[pl.BlockSpec((1, rank, width), at)] * 4,
            out_specs=pl.BlockSpec((4, rank, width), lambda i, *_: (0, i, 0)),
        ),
        out_shape=jax.ShapeDtypeStruct((4, requests * rank, width), BF16),
        compiler_params=params(),
        name="fetch_blocks",
    )(adapter_of, location, jnp.stack([replica, I32(held)]), *stores)


def down_kernel(counts, xa, xb, va, vb, own, other, out, blocks):
    rank = out.shape[1] // 2
    width = xa.shape[1]
    requests = own.shape[1] // rank
    first, packed = xa.shape[0], out.shape[0]
    blocks[...] = jnp.zeros_like(blocks)
    who = request_of(counts, iota((packed, 1), 0), packed)
    total = [jnp.zeros((first, 2 * rank), F32), jnp.zeros((packed - first, 2 * rank), F32)]
    for i in range(requests):
        rows = pl.ds(i * rank, rank)
        blocks[:rank, :width] = own[0, rows] + other[0, rows]
        blocks[rank:, width:] = own[1, rows] + other[1, rows]
        for k, (x, v, lo, hi) in enumerate(((xa, va, 0, first), (xb, vb, first, packed))):
            got = dot_t(x[...], blocks[:, :width]) + dot_t(v[...], blocks[:, width:])
            total[k] = total[k] + jnp.where(who[lo:hi] == i, got, 0.0)
    out[:first] = total[0]
    out[first:] = total[1]


def down(counts, xa, xb, va, vb, own, other):
    requests_rank, width = own.shape[1:]
    rank = requests_rank // 4
    packed = xa.shape[0] + xb.shape[0]
    half = (2, requests_rank, width)
    return pl.pallas_call(
        down_kernel,
        grid_spec=pltpu.PrefetchScalarGridSpec(
            num_scalar_prefetch=1,
            grid=(1,),
            in_specs=[whole(v.shape) for v in (xa, xb, va, vb)] + [whole(half)] * 2,
            out_specs=whole((packed, 2 * rank)),
            scratch_shapes=[pltpu.VMEM((2 * rank, 2 * width), BF16)],
        ),
        out_shape=jax.ShapeDtypeStruct((packed, 2 * rank), F32),
        compiler_params=params(),
        name="down_rows",
    )(counts, xa, xb, va, vb, own, other)


def up_kernel(counts, low, own, other, q_ref, o_ref, blocks):
    packed, both = low.shape
    rank = both // 2
    width = q_ref.shape[1]
    requests = own.shape[1] // rank
    blocks[...] = jnp.zeros_like(blocks)
    who = request_of(counts, iota((packed, 1), 0), packed)
    rows_low = low[...].astype(BF16).astype(F32)
    for i in range(requests):
        rows = pl.ds(i * rank, rank)
        blocks[pl.ds(2 * i * rank, rank), :width] = own[0, rows] + other[0, rows]
        blocks[pl.ds((2 * i + 1) * rank, rank), width:] = own[1, rows] + other[1, rows]
    wide = jnp.concatenate(
        [jnp.where(who == i, rows_low, 0.0).astype(BF16) for i in range(requests)], axis=1
    )
    q_ref[...] = adapter_scale * dot(wide, blocks[:, :width])
    o_ref[...] = adapter_scale * dot(wide, blocks[:, width:])


def up(counts, low, own, other):
    packed, both = low.shape
    requests_rank, width = own.shape[1:]
    half = (2, requests_rank, width)
    return pl.pallas_call(
        up_kernel,
        grid_spec=pltpu.PrefetchScalarGridSpec(
            num_scalar_prefetch=1,
            grid=(1,),
            in_specs=[whole(low.shape)]
            + [pl.BlockSpec(half, lambda *_: (1, 0, 0))] * 2,
            out_specs=[whole((packed, width))] * 2,
            scratch_shapes=[pltpu.VMEM((2 * requests_rank, 2 * width), BF16)],
        ),
        out_shape=[jax.ShapeDtypeStruct((packed, width), F32)] * 2,
        compiler_params=params(),
        name="up_rows",
    )(counts, low, own, other)


def shares_kernel(where, a_ref, b_ref, w_ref, cross_ref, own_ref, both_ref):
    j = pl.program_id(0)
    got = dot(a_ref[...], w_ref[...])
    both_ref[...] = dot(b_ref[...], w_ref[...])

    @pl.when(j < pl.num_programs(0) // 2)
    def _():
        cross_ref[...] = got

    @pl.when(j >= pl.num_programs(0) // 2)
    def _():
        own_ref[...] = got


def shares(owner, y, a, b, weight):
    width = a.shape[1]
    step = width // 2

    def column(j, where):
        return 2 * jnp.where(j < 2, 1 - where[1], where[1]) + j % 2

    return pl.pallas_call(
        shares_kernel,
        grid_spec=pltpu.PrefetchScalarGridSpec(
            num_scalar_prefetch=1,
            grid=(4,),
            in_specs=[
                whole(a.shape),
                whole(b.shape),
                pl.BlockSpec((width, step), lambda j, where: (0, 4 * where[0] + column(j, where))),
            ],
            out_specs=[
                pl.BlockSpec((a.shape[0], step), lambda j, where: (0, jnp.minimum(j, 1))),
                pl.BlockSpec((a.shape[0], step), lambda j, where: (0, jnp.maximum(j - 2, 0))),
                pl.BlockSpec((b.shape[0], step), lambda j, where: (0, column(j, where))),
            ],
        ),
        out_shape=[
            jax.ShapeDtypeStruct((a.shape[0], width), F32),
            jax.ShapeDtypeStruct((a.shape[0], width), F32),
            jax.ShapeDtypeStruct((b.shape[0], 2 * width), F32),
        ],
        compiler_params=params(),
        cost_estimate=pl.CostEstimate(
            flops=4 * (a.shape[0] + b.shape[0]) * width * width,
            bytes_accessed=4 * width * width + 2 * width * (a.shape[0] + b.shape[0]),
            transcendentals=0,
        ),
        name="shares",
    )(jnp.stack([owner, y]), a, b, weight)


def add_kernel(count, *refs):
    refs = refs[1:]
    pieces, weights, start, out = refs[:count], refs[count : 2 * count], refs[2 * count], refs[-1]
    total = start[...]
    for x, w in zip(pieces, weights):
        total = total + dot(x[...], w[...])
    out[...] = total


def add_products(start, pieces, at, weight):
    rows, columns = start.shape
    step = columns // 4
    count = len(pieces)

    def rows_of(i, depth, width):
        return pl.BlockSpec((depth, step), lambda j, at, i=i: (at[i], j))

    return pl.pallas_call(
        functools.partial(add_kernel, count),
        grid_spec=pltpu.PrefetchScalarGridSpec(
            num_scalar_prefetch=1,
            grid=(4,),
            in_specs=[whole(p.shape) for p in pieces]
            + [rows_of(i, p.shape[1], step) for i, p in enumerate(pieces)]
            + [pl.BlockSpec((rows, step), lambda j, at: (0, j))],
            out_specs=pl.BlockSpec((rows, step), lambda j, at: (0, j)),
        ),
        out_shape=jax.ShapeDtypeStruct((rows, columns), F32),
        compiler_params=params(),
        cost_estimate=pl.CostEstimate(
            flops=sum(2 * rows * columns * p.shape[1] for p in pieces),
            bytes_accessed=sum(2 * columns * p.shape[1] + 2 * rows * p.shape[1] for p in pieces),
            transcendentals=0,
        ),
        name="add_products",
    )(jnp.stack(at), *pieces, *([weight] * count), start)


def gather_z(x, edge):
    near_in, near_out = send(x, INNER), send(x, OUTWARD)
    one = jnp.where(edge, near_out, near_in)
    two = send(jnp.where(edge, x, one), SIDES)
    mid = send(two, INNER)
    out = send(mid, OUTWARD)
    three = jnp.where(edge, out, mid)
    return [x, one, two, three]


def narrow(value):
    return (value * SUM_SCALE).astype(F16)


def widen(value):
    return value.astype(F32) * (1.0 / SUM_SCALE)


def scatter_z(part, edge):
    r1 = send(narrow(part[0]), INWARD)
    r2 = send(narrow(part[0] + widen(r1)), INNER)
    r3 = send(narrow(part[1] + widen(r2)), SIDES)
    r4a = send(narrow(part[2]), INWARD)
    r4b = send(narrow(part[2] + widen(r3)), INNER)
    return part[3] + jnp.where(edge, widen(r3), widen(r4a) + widen(r4b))


def exchange(a_tok, b_tok, a_ctx, b_ctx, query_weight, output_weight, z, y):
    width = a_tok.shape[1]
    edge = (z == 0) | (z == 3)
    owners = [by_z(z, table) for table in (THREE, TWO, ONE, OWN)]
    shards = [by_z(z, table) for table in (OWN, ONE, TWO, THREE)]

    a_line = gather_z(a_tok, edge)
    b_pair = send(b_tok, Y_SWAP)
    parts = [shares(owner, y, a_ctx, b_ctx, output_weight) for owner in owners]
    a_from_y = [send(narrow(cross), Y_SWAP) for cross, _, _ in parts]
    b_sum = scatter_z([both for _, _, both in parts], edge)
    a_sum = scatter_z([own + widen(got) for (_, own, _), got in zip(parts, a_from_y)], edge)
    b_both = jnp.concatenate(
        [jnp.where(y == 0, b_tok, b_pair), jnp.where(y == 0, b_pair, b_tok)], axis=1
    )
    b_line = gather_z(b_both, edge)
    a_cross = [send(v, Y_SWAP) for v in a_line]
    low_half, high_half = b_sum[:, :width], b_sum[:, width:]
    b_mine = jnp.where(y == 0, low_half, high_half)
    b_theirs = jnp.where(y == 0, high_half, low_half)
    b_sum = b_mine + widen(send(narrow(b_theirs), Y_SWAP))

    columns = query_weight.shape[1]
    a_q = jnp.zeros((a_tok.shape[0], columns), F32)
    b_q = jnp.zeros((b_tok.shape[0], columns), F32)
    a_q = add_products(a_q, a_line, [2 * s + y for s in shards], query_weight)
    a_q = add_products(a_q, a_cross, [2 * s + 1 - y for s in shards], query_weight)
    b_q = add_products(b_q, b_line, shards, query_weight)
    return a_q, b_q, a_sum, b_sum


def sum_over_tensor(part):
    total = part
    for pairs in (Y_SWAP, SIDES, FAR):
        mine = (total * DOWN_SCALE).astype(F16)
        moved = send(mine, pairs)
        total = (mine.astype(F32) + moved.astype(F32)) * (1.0 / DOWN_SCALE)
    return total


def make(mesh):
    grid = mesh.shape["tensor"] == 8

    def local(
        tokens, context, query_weight, output_weight,
        store_aq, store_bq, store_ao, store_bo,
        adapter_of, location, token_count,
    ):
        rows, width = tokens.shape
        per = rows // REQUEST_LENGTH
        packed = rows * 3 // 4
        spare = rows - packed
        first = packed - spare
        replica = lax.axis_index("replica")
        at = lax.axis_index("tensor")
        z, y = at // 2, at % 2
        flip = jnp.where(replica == 0, token_count, jnp.roll(token_count, per))
        counts = jnp.concatenate([flip, replica[None]]).astype(I32)

        tok_a, tok_b, tok_c = pack(counts, tokens, packed)
        ctx_a, ctx_b, ctx_c = pack(counts, context, packed)
        tok_b = tok_b + other_replica(tok_c)
        ctx_b = ctx_b + other_replica(ctx_c)

        own = fetch((store_aq, store_ao, store_bq, store_bo), adapter_of, location, replica)
        other = other_replica(own)
        parts = down(counts, tok_a, tok_b, ctx_a, ctx_b, own, other)

        if grid:
            low = sum_over_tensor(parts)
            q_a, q_b, o_a, o_b = exchange(
                tok_a, tok_b, ctx_a, ctx_b, query_weight, output_weight, z, y
            )
        else:
            low = lax.psum(parts, "tensor")
            tok = jnp.concatenate([tok_a, tok_b])
            ctx = jnp.concatenate([ctx_a, ctx_b])
            base_q = dot(lax.all_gather(tok, "tensor", axis=1, tiled=True), query_weight)
            base_o = lax.psum_scatter(
                dot(ctx, output_weight), "tensor", scatter_dimension=1, tiled=True
            )
            q_a, q_b, o_a, o_b = base_q[:first], base_q[first:], base_o[:first], base_o[first:]

        up_q, up_o = up(counts, low, own, other)
        q_a, q_b = (q_a + up_q[:first]).astype(BF16), (q_b + up_q[first:]).astype(BF16)
        o_a, o_b = (o_a + up_o[:first]).astype(BF16), (o_b + up_o[first:]).astype(BF16)
        return tuple(
            unpack(counts, rows, (q_a, q_b, other_replica(q_b), o_a, o_b, other_replica(o_b)))
        )

    return local


def solution(mesh):
    return jax.shard_map(
        make(mesh),
        mesh=mesh,
        in_specs=(
            P(("groups", "replica"), "tensor"),
            P(("groups", "replica"), "tensor"),
            P(None, "tensor"),
            P("tensor", None),
            P(("groups", "replica"), None, "tensor"),
            P(("groups", "replica"), None, "tensor"),
            P(("groups", "replica"), None, "tensor"),
            P(("groups", "replica"), None, "tensor"),
            P("groups"),
            P("groups"),
            P("groups"),
        ),
        out_specs=(P(("groups", "replica"), "tensor"), P(("groups", "replica"), "tensor")),
        check_vma=False,
    )
```

```python
import functools

import jax
import jax.numpy as jnp
from jax import lax
from jax.experimental import pallas as pl
from jax.experimental.pallas import tpu as pltpu
from jax.sharding import PartitionSpec as P

REQUEST_LENGTH = 256


adapter_scale = 0.5

SUM_SCALE = 8.0
DOWN_SCALE = 16.0

BF16 = jnp.bfloat16
F16 = jnp.float16
F32 = jnp.float32
I32 = jnp.int32

SMALL = 16 * 1024 * 1024
LARGE = 48 * 1024 * 1024


def ring_order(size):
    if size == 8:
        return [0, 2, 4, 6, 7, 5, 3, 1]
    return list(range(size))


def send(value, pairs, name):
    with jax.named_scope(name):
        return lax.ppermute(value, "tensor", pairs)


def other_replica(value):
    return lax.ppermute(value, "replica", [(0, 1), (1, 0)])


def dot(a, b):
    return jnp.dot(a, b, preferred_element_type=F32)


def dot_t(a, b):
    return lax.dot_general(a, b, (((1,), (1,)), ((), ())), preferred_element_type=F32)


def look_up(index, table):
    out = I32(table[0])
    for i, entry in enumerate(table[1:], 1):
        out = jnp.where(index == i, I32(entry), out)
    return out


def whole(shape):
    return pl.BlockSpec(shape, lambda *_: (0,) * len(shape))


def params(limit=SMALL):
    return pltpu.CompilerParams(dimension_semantics=("arbitrary",), vmem_limit_bytes=limit)


def iota(shape, dim):
    return lax.broadcasted_iota(I32, shape, dim)


def lengths(counts, place):
    mine, theirs = 2 * place[0], 2 - 2 * place[0]
    return counts[mine], counts[mine + 1], counts[theirs], counts[theirs + 1]


def select_rows(home, x):
    hot = iota((home.shape[0], x.shape[0]), 1) == home
    return dot(hot.astype(F32).astype(BF16), x[...])


def home_of(position, live, c_a):
    home = jnp.where(position < c_a, position, REQUEST_LENGTH + position - c_a)
    return jnp.where(live, home, -1)


def spare_kernel(counts, place, x_ref, v_ref, out):
    rows, spare = x_ref.shape[0], out.shape[0] // 2
    packed = rows - spare
    c_a, c_b, d_a, d_b = lengths(counts, place)
    seat = iota((spare, 1), 0) + packed - spare - d_a - d_b
    home = home_of(packed + seat, seat >= 0, c_a)
    out[:spare] = select_rows(home, x_ref).astype(BF16)
    out[spare:] = select_rows(home, v_ref).astype(BF16)


def spare_rows(counts, place, x, v, spare):
    shape = (2 * spare, x.shape[1])
    return pl.pallas_call(
        spare_kernel,
        grid_spec=pltpu.PrefetchScalarGridSpec(
            num_scalar_prefetch=2,
            grid=(1,),
            in_specs=[whole(x.shape)] * 2,
            out_specs=whole(shape),
        ),
        out_shape=jax.ShapeDtypeStruct(shape, BF16),
        compiler_params=params(),
        name="spare_rows",
    )(counts, place, x, v)


def pack_kernel(counts, place, x_ref, moved_ref, out):
    packed, spare = out.shape[0], moved_ref.shape[0]
    first = packed - spare
    c_a, c_b, _, _ = lengths(counts, place)
    slot = iota((packed, 1), 0)
    here = select_rows(home_of(slot, slot < c_a + c_b, c_a), x_ref)
    out[:first] = here[:first].astype(BF16)
    out[first:] = (here[first:] + moved_ref[...].astype(F32)).astype(BF16)


def pack(counts, place, x, moved, which):
    rows, width = x.shape
    spare = moved.shape[0] // 2
    shape = (rows - spare, width)
    return pl.pallas_call(
        pack_kernel,
        grid_spec=pltpu.PrefetchScalarGridSpec(
            num_scalar_prefetch=2,
            grid=(1,),
            in_specs=[whole(x.shape), pl.BlockSpec((spare, width), lambda *_: (which, 0))],
            out_specs=whole(shape),
        ),
        out_shape=jax.ShapeDtypeStruct(shape, BF16),
        compiler_params=params(),
        name="pack_rows",
    )(counts, place, x, moved)


def unpack_kernel(counts, place, x_ref, spare_ref, out):
    rows = out.shape[0]
    packed, spare = x_ref.shape[0], spare_ref.shape[0]
    first = packed - spare
    c_a, c_b, d_a, d_b = lengths(counts, place)
    n_theirs = d_a + d_b
    row = iota((rows, 1), 0)
    late = row >= REQUEST_LENGTH
    offset = jnp.where(late, row - REQUEST_LENGTH, row)
    position = offset + jnp.where(late, c_a, 0)
    target = jnp.where(position < packed, position, position + n_theirs - first)
    target = jnp.where(offset < jnp.where(late, c_b, c_a), target, -1)
    hot = (iota((rows, rows), 1) == target).astype(F32).astype(BF16)
    out[...] = (dot(hot[:, :packed], x_ref[...]) + dot(hot[:, packed:], spare_ref[...])).astype(BF16)


def unpack(counts, place, rows, parts):
    shape = (rows, parts[0].shape[1])
    return pl.pallas_call(
        unpack_kernel,
        grid_spec=pltpu.PrefetchScalarGridSpec(
            num_scalar_prefetch=2,
            grid=(1,),
            in_specs=[whole(p.shape) for p in parts],
            out_specs=whole(shape),
        ),
        out_shape=jax.ShapeDtypeStruct(shape, BF16),
        compiler_params=params(),
        name="unpack_rows",
    )(counts, place, *parts)


def request_of(counts, place, slot, packed):
    c_a, c_b, d_a, _ = lengths(counts, place)
    n_mine, replica = c_a + c_b, place[0]
    own = slot < n_mine
    seat = jnp.where(own, slot, packed + slot - n_mine)
    mine = 2 * replica + (seat >= c_a).astype(I32)
    theirs = 2 * (1 - replica) + (seat >= d_a).astype(I32)
    return jnp.where(own, mine, theirs)


def fetch_kernel(held, adapter_of, location, place, *refs):
    stores, out = refs[:4], refs[4]
    slot = location[adapter_of[pl.program_id(0)]] - place[0] * held
    mine = (slot >= 0) & (slot < held)
    for k, table in enumerate(stores):
        block = table[0]
        out[k] = jnp.where(mine, block, jnp.zeros_like(block))


def fetch(stores, adapter_of, location, place):
    held, rank, width = stores[0].shape
    requests = adapter_of.shape[0]

    def at(i, adapter_of, location, place):
        slot = location[adapter_of[i]] - place[0] * held
        return jnp.clip(slot, 0, held - 1), 0, 0

    return pl.pallas_call(
        functools.partial(fetch_kernel, held),
        grid_spec=pltpu.PrefetchScalarGridSpec(
            num_scalar_prefetch=3,
            grid=(requests,),
            in_specs=[pl.BlockSpec((1, rank, width), at)] * 4,
            out_specs=pl.BlockSpec((4, rank, width), lambda i, *_: (0, i, 0)),
        ),
        out_shape=jax.ShapeDtypeStruct((4, requests * rank, width), BF16),
        compiler_params=params(LARGE),
        name="fetch_blocks",
    )(adapter_of, location, place, *stores)


def down_kernel(counts, place, x, v, own, other, out, blocks):
    rank = out.shape[1] // 2
    packed, width = x.shape
    requests = own.shape[1] // rank
    blocks[...] = jnp.zeros_like(blocks)
    who = request_of(counts, place, iota((packed, 1), 0), packed)
    total = jnp.zeros(out.shape, F32)
    for i in range(requests):
        rows = pl.ds(i * rank, rank)
        blocks[:rank, :width] = own[0, rows] + other[0, rows]
        blocks[rank:, width:] = own[1, rows] + other[1, rows]
        got = dot_t(x[...], blocks[:, :width]) + dot_t(v[...], blocks[:, width:])
        total = total + jnp.where(who == i, got, 0.0)
    out[...] = total


def down(counts, place, x, v, own, other):
    requests_rank, width = own.shape[1:]
    rank = requests_rank // 4
    packed = x.shape[0]
    half = (2, requests_rank, width)
    return pl.pallas_call(
        down_kernel,
        grid_spec=pltpu.PrefetchScalarGridSpec(
            num_scalar_prefetch=2,
            grid=(1,),
            in_specs=[whole(v.shape) for v in (x, v)] + [whole(half)] * 2,
            out_specs=whole((packed, 2 * rank)),
            scratch_shapes=[pltpu.VMEM((2 * rank, 2 * width), BF16)],
        ),
        out_shape=jax.ShapeDtypeStruct((packed, 2 * rank), F32),
        compiler_params=params(),
        name="down_rows",
    )(counts, place, x, v, own, other)


def up_kernel(counts, place, low, own, other, q_ref, o_ref, blocks):
    packed, both = low.shape
    rank = both // 2
    width = q_ref.shape[1]
    requests = own.shape[1] // rank
    blocks[...] = jnp.zeros_like(blocks)
    who = request_of(counts, place, iota((packed, 1), 0), packed)
    rows_low = low[...].astype(BF16).astype(F32)
    for i in range(requests):
        rows = pl.ds(i * rank, rank)
        blocks[pl.ds(2 * i * rank, rank), :width] = own[0, rows] + other[0, rows]
        blocks[pl.ds((2 * i + 1) * rank, rank), width:] = own[1, rows] + other[1, rows]
    wide = jnp.concatenate(
        [jnp.where(who == i, rows_low, 0.0).astype(BF16) for i in range(requests)], axis=1
    )
    q_ref[...] = adapter_scale * dot(wide, blocks[:, :width])
    o_ref[...] = adapter_scale * dot(wide, blocks[:, width:])


def up(counts, place, low, own, other):
    packed, both = low.shape
    requests_rank, width = own.shape[1:]
    half = (2, requests_rank, width)
    return pl.pallas_call(
        up_kernel,
        grid_spec=pltpu.PrefetchScalarGridSpec(
            num_scalar_prefetch=2,
            grid=(1,),
            in_specs=[whole(low.shape)]
            + [pl.BlockSpec(half, lambda *_: (1, 0, 0))] * 2,
            out_specs=[whole((packed, width))] * 2,
            scratch_shapes=[pltpu.VMEM((2 * requests_rank, 2 * width), BF16)],
        ),
        out_shape=[jax.ShapeDtypeStruct((packed, width), F32)] * 2,
        compiler_params=params(),
        name="up_rows",
    )(counts, place, low, own, other)


def shares_kernel(where, x_ref, w_ref, out):
    out[0] = dot(x_ref[...], w_ref[...])


def shares(where, start, count, x, weight):
    rows, width = x.shape
    return pl.pallas_call(
        shares_kernel,
        grid_spec=pltpu.PrefetchScalarGridSpec(
            num_scalar_prefetch=1,
            grid=(count,),
            in_specs=[
                whole(x.shape),
                pl.BlockSpec((width, width), lambda i, where: (0, where[start + i])),
            ],
            out_specs=pl.BlockSpec((1, rows, width), lambda i, where: (i, 0, 0)),
        ),
        out_shape=jax.ShapeDtypeStruct((count, rows, width), F32),
        compiler_params=params(LARGE),
        name="shares",
    )(where, x, weight)


def add_kernel(pieces, where, *refs):
    xs, ws, extra, out = refs[:pieces], refs[pieces : 2 * pieces], refs[2 * pieces : -1], refs[-1]
    total = dot(xs[0][...], ws[0][...])
    for x, w in zip(xs[1:], ws[1:]):
        total = total + dot(x[...], w[...])
    for more in extra:
        total = total + more[...]
    out[...] = total.astype(out.dtype)


def add_products(where, pieces, at, weight, addends, dtype=F32):
    rows, width = pieces[0].shape
    columns = weight.shape[1]
    step = columns // 2

    def rows_of(i):
        return pl.BlockSpec((width, step), lambda j, where: (where[at[i]], j))

    tall = pl.BlockSpec((rows, step), lambda j, where: (0, j))
    return pl.pallas_call(
        functools.partial(add_kernel, len(pieces)),
        grid_spec=pltpu.PrefetchScalarGridSpec(
            num_scalar_prefetch=1,
            grid=(2,),
            in_specs=[whole(p.shape) for p in pieces]
            + [rows_of(i) for i in range(len(pieces))]
            + [tall] * len(addends),
            out_specs=tall,
        ),
        out_shape=jax.ShapeDtypeStruct((rows, columns), dtype),
        compiler_params=params(LARGE),
        name="add_products",
    )(where, *pieces, *([weight] * len(pieces)), *addends)


def narrow(value):
    return (value * SUM_SCALE).astype(F16)


def widen(value):
    return value.astype(F32) * (1.0 / SUM_SCALE)


def tie(value, *others):
    return lax.optimization_barrier((value, others))[0]


def swap_down(total, bit, size):
    mine = (total * DOWN_SCALE).astype(F16)
    moved = send(mine, [(t, t ^ bit) for t in range(size)], "down_swap")
    return (mine.astype(F32) + moved.astype(F32)) * (1.0 / DOWN_SCALE)


def make(mesh):
    size = mesh.shape["tensor"]
    order = ring_order(size)
    steps = size // 2
    following = [(order[p], order[(p + 1) % size]) for p in range(size)]
    preceding = [(b, a) for a, b in following]
    offsets = [0] + [sign * d for d in range(1, steps) for sign in (1, -1)] + [steps]
    place_of = [order.index(t) for t in range(size)]

    def local(
        tokens, context, query_weight, output_weight,
        store_aq, store_bq, store_ao, store_bo,
        adapter_of, location, token_count,
    ):
        rows, width = tokens.shape
        packed = rows * 3 // 4
        spare = rows - packed
        half = packed // 2
        at = lax.axis_index("tensor")
        place = jnp.stack([lax.axis_index("replica")]).astype(I32)
        counts = token_count
        where = jnp.stack(
            [look_up(at, [order[(p + d) % size] for p in place_of]) for d in offsets]
        )

        moved = other_replica(spare_rows(counts, place, tokens, context, spare))
        mine = fetch((store_aq, store_ao, store_bq, store_bo), adapter_of, location, place)
        tok = pack(counts, place, tokens, tie(moved, mine), 0)
        ahead, behind = send(tok, following, "gather_up_1"), send(tok, preceding, "gather_down_1")
        ctx = pack(counts, place, tie(context, tok), moved, 1)
        far = narrow(shares(where, size - 1, 1, ctx, output_weight)[0])
        up_sum = send(far[:half], following, "scatter_up_1")
        down_sum = send(far[half:], preceding, "scatter_down_1")
        theirs = other_replica(mine)
        near = list(shares(where, size - 3, 2, tie(ctx, far), output_weight))

        q, bit = None, 1
        for step in range(1, steps):
            up_sum, down_sum = lax.optimization_barrier((tie(up_sum, near), down_sum))
            up_share, down_share = near[0], near[1]
            if step == 1:
                up_out = jnp.concatenate([up_share[:half] + widen(up_sum), up_share[half:]])
                down_out = jnp.concatenate([down_share[:half], down_share[half:] + widen(down_sum)])
            else:
                up_out, down_out = up_share + widen(up_sum), down_share + widen(down_sum)
            up_out, down_out = narrow(up_out), narrow(down_out)
            up_sum = send(up_out, following, f"scatter_up_{step + 1}")
            down_sum = send(down_out, preceding, f"scatter_down_{step + 1}")
            got_up, got_down = lax.optimization_barrier((tie(ahead, up_out, down_out), behind))
            if step < steps - 1:
                ahead = send(got_up, following, f"gather_up_{step + 1}")
                behind = send(got_down, preceding, f"gather_down_{step + 1}")
            else:
                ahead = send(got_up[:half], following, f"gather_up_{step + 1}")
                behind = send(got_down[half:], preceding, f"gather_down_{step + 1}")
            ready = got_up
            if step == 1:
                theirs = tie(theirs, up_out)
                parts = down(counts, place, tok, ctx, tie(mine, ready), theirs)
                ready = parts
            if bit < size:
                parts = swap_down(tie(parts, ready), bit, size)
                bit *= 2
            if step == 1:
                rest = shares(where, 0, size - 3, tie(ctx, ready), output_weight)
                ready = rest
                pieces, at_pieces, sofar = [tok, got_down, got_up], [0, 1, 2], []
            else:
                pieces, at_pieces, sofar = [got_down, got_up], [2 * step - 1, 2 * step], [q]
            pieces[0] = tie(pieces[0], ready)
            q = add_products(where, pieces, at_pieces, query_weight, sofar)
            d = steps - step - 1
            near = [tie(rest[2 * d - 1], q), rest[2 * d]]
        while bit < size:
            parts = swap_down(tie(parts, q), bit, size)
            bit *= 2
        up_q, up_o = up(counts, place, tie(parts, q), mine, theirs)
        got_up, got_down = lax.optimization_barrier((tie(ahead, up_q), behind))
        last = jnp.concatenate([got_up, got_down])
        q = add_products(where, [last], [size - 1], query_weight, [q, up_q], BF16)
        q_m = other_replica(q[packed - spare :])
        up_sum, down_sum = lax.optimization_barrier((tie(up_sum, q), down_sum))
        o = (rest[0] + widen(up_sum) + widen(down_sum) + up_o).astype(BF16)
        o_m = other_replica(o[packed - spare :])
        queries = unpack(counts, place, rows, (q, tie(q_m, o)))
        attended = unpack(counts, place, rows, (o, tie(o_m, queries)))
        return queries, attended

    return local


def solution(mesh):
    return jax.shard_map(
        make(mesh),
        mesh=mesh,
        in_specs=(
            P(("groups", "replica"), "tensor"),
            P(("groups", "replica"), "tensor"),
            P(None, "tensor"),
            P("tensor", None),
            P(("groups", "replica"), None, "tensor"),
            P(("groups", "replica"), None, "tensor"),
            P(("groups", "replica"), None, "tensor"),
            P(("groups", "replica"), None, "tensor"),
            P("groups"),
            P("groups"),
            P("groups"),
        ),
        out_specs=(P(("groups", "replica"), "tensor"), P(("groups", "replica"), "tensor")),
        check_vma=False,
    )
```

```python
import functools

import jax
import jax.numpy as jnp
from jax import lax
from jax.experimental import pallas as pl
from jax.experimental.pallas import tpu as pltpu
from jax.sharding import PartitionSpec as P

REQUEST_LENGTH = 256


adapter_scale = 0.5

SUM_SCALE = 8.0
DOWN_SCALE = 16.0

BF16 = jnp.bfloat16
F16 = jnp.float16
F32 = jnp.float32
I32 = jnp.int32

SMALL = 16 * 1024 * 1024
LARGE = 48 * 1024 * 1024


def ring_order(size):
    if size == 8:
        return [0, 2, 4, 6, 7, 5, 3, 1]
    return list(range(size))


def send(value, pairs, name):
    with jax.named_scope(name):
        return lax.ppermute(value, "tensor", pairs)


def other_replica(value):
    return lax.ppermute(value, "replica", [(0, 1), (1, 0)])


def dot(a, b):
    return jnp.dot(a, b, preferred_element_type=F32)


def dot_t(a, b):
    return lax.dot_general(a, b, (((1,), (1,)), ((), ())), preferred_element_type=F32)


def look_up(index, table):
    out = I32(table[0])
    for i, entry in enumerate(table[1:], 1):
        out = jnp.where(index == i, I32(entry), out)
    return out


def whole(shape):
    return pl.BlockSpec(shape, lambda *_: (0,) * len(shape))


def params(limit=SMALL):
    return pltpu.CompilerParams(dimension_semantics=("arbitrary",), vmem_limit_bytes=limit)


def iota(shape, dim):
    return lax.broadcasted_iota(I32, shape, dim)


def lengths(counts, place):
    mine, theirs = 2 * place[0], 2 - 2 * place[0]
    return counts[mine], counts[mine + 1], counts[theirs], counts[theirs + 1]


def select_rows(home, x):
    hot = iota((home.shape[0], x.shape[0]), 1) == home
    return dot(hot.astype(F32).astype(BF16), x[...])


def home_of(position, live, c_a):
    home = jnp.where(position < c_a, position, REQUEST_LENGTH + position - c_a)
    return jnp.where(live, home, -1)


def spare_kernel(counts, place, x_ref, v_ref, out):
    rows, spare = x_ref.shape[0], out.shape[0] // 2
    packed = rows - spare
    c_a, c_b, d_a, d_b = lengths(counts, place)
    seat = iota((spare, 1), 0) + packed - spare - d_a - d_b
    home = home_of(packed + seat, seat >= 0, c_a)
    out[:spare] = select_rows(home, x_ref).astype(BF16)
    out[spare:] = select_rows(home, v_ref).astype(BF16)


def spare_rows(counts, place, x, v, spare):
    shape = (2 * spare, x.shape[1])
    return pl.pallas_call(
        spare_kernel,
        grid_spec=pltpu.PrefetchScalarGridSpec(
            num_scalar_prefetch=2,
            grid=(1,),
            in_specs=[whole(x.shape)] * 2,
            out_specs=whole(shape),
        ),
        out_shape=jax.ShapeDtypeStruct(shape, BF16),
        compiler_params=params(LARGE),
        name="spare_rows",
    )(counts, place, x, v)


def pack_kernel(counts, place, x_ref, moved_ref, out):
    packed, spare = out.shape[0], moved_ref.shape[0]
    first = packed - spare
    c_a, c_b, _, _ = lengths(counts, place)
    slot = iota((packed, 1), 0)
    here = select_rows(home_of(slot, slot < c_a + c_b, c_a), x_ref)
    out[:first] = here[:first].astype(BF16)
    out[first:] = (here[first:] + moved_ref[...].astype(F32)).astype(BF16)


def pack(counts, place, x, moved, which):
    rows, width = x.shape
    spare = moved.shape[0] // 2
    shape = (rows - spare, width)
    return pl.pallas_call(
        pack_kernel,
        grid_spec=pltpu.PrefetchScalarGridSpec(
            num_scalar_prefetch=2,
            grid=(1,),
            in_specs=[whole(x.shape), pl.BlockSpec((spare, width), lambda *_: (which, 0))],
            out_specs=whole(shape),
        ),
        out_shape=jax.ShapeDtypeStruct(shape, BF16),
        compiler_params=params(LARGE),
        name="pack_rows",
    )(counts, place, x, moved)


def unpack_kernel(counts, place, x_ref, spare_ref, out):
    rows = out.shape[0]
    packed, spare = x_ref.shape[0], spare_ref.shape[0]
    first = packed - spare
    c_a, c_b, d_a, d_b = lengths(counts, place)
    n_theirs = d_a + d_b
    row = iota((rows, 1), 0)
    late = row >= REQUEST_LENGTH
    offset = jnp.where(late, row - REQUEST_LENGTH, row)
    position = offset + jnp.where(late, c_a, 0)
    target = jnp.where(position < packed, position, position + n_theirs - first)
    target = jnp.where(offset < jnp.where(late, c_b, c_a), target, -1)
    hot = (iota((rows, rows), 1) == target).astype(F32).astype(BF16)
    out[...] = (dot(hot[:, :packed], x_ref[...]) + dot(hot[:, packed:], spare_ref[...])).astype(BF16)


def unpack(counts, place, rows, parts):
    shape = (rows, parts[0].shape[1])
    return pl.pallas_call(
        unpack_kernel,
        grid_spec=pltpu.PrefetchScalarGridSpec(
            num_scalar_prefetch=2,
            grid=(1,),
            in_specs=[whole(p.shape) for p in parts],
            out_specs=whole(shape),
        ),
        out_shape=jax.ShapeDtypeStruct(shape, BF16),
        compiler_params=params(),
        name="unpack_rows",
    )(counts, place, *parts)


def request_of(counts, place, slot, packed):
    c_a, c_b, d_a, _ = lengths(counts, place)
    n_mine, replica = c_a + c_b, place[0]
    own = slot < n_mine
    seat = jnp.where(own, slot, packed + slot - n_mine)
    mine = 2 * replica + (seat >= c_a).astype(I32)
    theirs = 2 * (1 - replica) + (seat >= d_a).astype(I32)
    return jnp.where(own, mine, theirs)


def fetch_kernel(held, adapter_of, location, place, *refs):
    stores, out = refs[:4], refs[-1]
    slot = location[adapter_of[pl.program_id(0)]] - place[0] * held
    mine = (slot >= 0) & (slot < held)
    for k, table in enumerate(stores):
        block = table[0]
        out[k] = jnp.where(mine, block, jnp.zeros_like(block))


def fetch(stores, adapter_of, location, place, after):
    held, rank, width = stores[0].shape
    requests = adapter_of.shape[0]

    def at(i, adapter_of, location, place):
        slot = location[adapter_of[i]] - place[0] * held
        return jnp.clip(slot, 0, held - 1), 0, 0

    return pl.pallas_call(
        functools.partial(fetch_kernel, held),
        grid_spec=pltpu.PrefetchScalarGridSpec(
            num_scalar_prefetch=3,
            grid=(requests,),
            in_specs=[pl.BlockSpec((1, rank, width), at)] * 4 + [pl.BlockSpec(memory_space=pl.ANY)],
            out_specs=pl.BlockSpec((4, rank, width), lambda i, *_: (0, i, 0)),
        ),
        out_shape=jax.ShapeDtypeStruct((4, requests * rank, width), BF16),
        compiler_params=params(LARGE),
        name="fetch_blocks",
    )(adapter_of, location, place, *stores, after)


def down_kernel(counts, place, x, v, own, other, out, blocks):
    rank = out.shape[1] // 2
    packed, width = x.shape
    requests = own.shape[1] // rank
    blocks[...] = jnp.zeros_like(blocks)
    who = request_of(counts, place, iota((packed, 1), 0), packed)
    total = jnp.zeros(out.shape, F32)
    for i in range(requests):
        rows = pl.ds(i * rank, rank)
        blocks[:rank, :width] = own[0, rows] + other[0, rows]
        blocks[rank:, width:] = own[1, rows] + other[1, rows]
        got = dot_t(x[...], blocks[:, :width]) + dot_t(v[...], blocks[:, width:])
        total = total + jnp.where(who == i, got, 0.0)
    out[...] = total


def down(counts, place, x, v, own, other):
    requests_rank, width = own.shape[1:]
    rank = requests_rank // 4
    packed = x.shape[0]
    half = (2, requests_rank, width)
    return pl.pallas_call(
        down_kernel,
        grid_spec=pltpu.PrefetchScalarGridSpec(
            num_scalar_prefetch=2,
            grid=(1,),
            in_specs=[whole(v.shape) for v in (x, v)] + [whole(half)] * 2,
            out_specs=whole((packed, 2 * rank)),
            scratch_shapes=[pltpu.VMEM((2 * rank, 2 * width), BF16)],
        ),
        out_shape=jax.ShapeDtypeStruct((packed, 2 * rank), F32),
        compiler_params=params(),
        name="down_rows",
    )(counts, place, x, v, own, other)


def up_kernel(counts, place, low, own, other, q_ref, o_ref, blocks):
    packed, both = low.shape
    rank = both // 2
    width = q_ref.shape[1]
    requests = own.shape[1] // rank
    blocks[...] = jnp.zeros_like(blocks)
    who = request_of(counts, place, iota((packed, 1), 0), packed)
    rows_low = low[...].astype(BF16).astype(F32)
    for i in range(requests):
        rows = pl.ds(i * rank, rank)
        blocks[pl.ds(2 * i * rank, rank), :width] = own[0, rows] + other[0, rows]
        blocks[pl.ds((2 * i + 1) * rank, rank), width:] = own[1, rows] + other[1, rows]
    wide = jnp.concatenate(
        [jnp.where(who == i, rows_low, 0.0).astype(BF16) for i in range(requests)], axis=1
    )
    q_ref[...] = adapter_scale * dot(wide, blocks[:, :width])
    o_ref[...] = adapter_scale * dot(wide, blocks[:, width:])


def up(counts, place, low, own, other):
    packed, both = low.shape
    requests_rank, width = own.shape[1:]
    half = (2, requests_rank, width)
    return pl.pallas_call(
        up_kernel,
        grid_spec=pltpu.PrefetchScalarGridSpec(
            num_scalar_prefetch=2,
            grid=(1,),
            in_specs=[whole(low.shape)]
            + [pl.BlockSpec(half, lambda *_: (1, 0, 0))] * 2,
            out_specs=[whole((packed, width))] * 2,
            scratch_shapes=[pltpu.VMEM((2 * requests_rank, 2 * width), BF16)],
        ),
        out_shape=[jax.ShapeDtypeStruct((packed, width), F32)] * 2,
        compiler_params=params(),
        name="up_rows",
    )(counts, place, low, own, other)


def shares_kernel(where, x_ref, w_ref, out):
    out[0] = dot(x_ref[...], w_ref[...])


def shares(where, start, count, x, weight):
    rows, width = x.shape
    return pl.pallas_call(
        shares_kernel,
        grid_spec=pltpu.PrefetchScalarGridSpec(
            num_scalar_prefetch=1,
            grid=(count,),
            in_specs=[
                whole(x.shape),
                pl.BlockSpec((width, width), lambda i, where: (0, where[start + i])),
            ],
            out_specs=pl.BlockSpec((1, rows, width), lambda i, where: (i, 0, 0)),
        ),
        out_shape=jax.ShapeDtypeStruct((count, rows, width), F32),
        compiler_params=params(LARGE),
        name="shares",
    )(where, x, weight)


def add_kernel(pieces, where, *refs):
    xs, ws, extra, out = refs[:pieces], refs[pieces : 2 * pieces], refs[2 * pieces : -1], refs[-1]
    total = dot(xs[0][...], ws[0][...])
    for x, w in zip(xs[1:], ws[1:]):
        total = total + dot(x[...], w[...])
    for more in extra:
        total = total + more[...]
    out[...] = total.astype(out.dtype)


def add_products(where, pieces, at, weight, addends, dtype=F32):
    rows, width = pieces[0].shape
    columns = weight.shape[1]
    step = columns // 2

    def rows_of(i):
        return pl.BlockSpec((width, step), lambda j, where: (where[at[i]], j))

    tall = pl.BlockSpec((rows, step), lambda j, where: (0, j))
    return pl.pallas_call(
        functools.partial(add_kernel, len(pieces)),
        grid_spec=pltpu.PrefetchScalarGridSpec(
            num_scalar_prefetch=1,
            grid=(2,),
            in_specs=[whole(p.shape) for p in pieces]
            + [rows_of(i) for i in range(len(pieces))]
            + [tall] * len(addends),
            out_specs=tall,
        ),
        out_shape=jax.ShapeDtypeStruct((rows, columns), dtype),
        compiler_params=params(LARGE),
        name="add_products",
    )(where, *pieces, *([weight] * len(pieces)), *addends)


def narrow(value):
    return (value * SUM_SCALE).astype(F16)


def widen(value):
    return value.astype(F32) * (1.0 / SUM_SCALE)


def tie(value, *others):
    return lax.optimization_barrier((value, others))[0]


def swap(total, bit, size):
    mine = (total * DOWN_SCALE).astype(F16)
    return send(mine, [(t, t ^ bit) for t in range(size)], f"down_sums_{bit}"), mine


def meet(moved, mine):
    return (mine.astype(F32) + moved.astype(F32)) * (1.0 / DOWN_SCALE)


def make(mesh):
    size = mesh.shape["tensor"]
    order = ring_order(size)
    steps = size // 2
    following = [(order[p], order[(p + 1) % size]) for p in range(size)]
    preceding = [(b, a) for a, b in following]
    offsets = [0] + [sign * d for d in range(1, steps) for sign in (1, -1)] + [steps]
    place_of = [order.index(t) for t in range(size)]

    def local(
        tokens, context, query_weight, output_weight,
        store_aq, store_bq, store_ao, store_bo,
        adapter_of, location, token_count,
    ):
        rows, width = tokens.shape
        packed = rows * 3 // 4
        spare = rows - packed
        half = packed // 2
        at = lax.axis_index("tensor")
        place = jnp.stack([lax.axis_index("replica")]).astype(I32)
        counts = token_count
        where = jnp.stack(
            [look_up(at, [order[(p + d) % size] for p in place_of]) for d in offsets]
        )

        handed = spare_rows(counts, place, tokens, context, spare)
        moved = other_replica(handed)
        tok = pack(counts, place, tokens, moved, 0)
        ahead, behind = send(tok, following, "gather_up_1"), send(tok, preceding, "gather_down_1")
        ctx = pack(counts, tie(place, tok), context, moved, 1)
        stores = (store_aq, store_ao, store_bq, store_bo)
        mine = fetch(stores, adapter_of, location, place, ctx)
        theirs = other_replica(mine)
        far = narrow(shares(tie(where, mine), size - 1, 1, ctx, output_weight)[0])
        up_sum = send(far[:half], following, "scatter_up_1")
        down_sum = send(far[half:], preceding, "scatter_down_1")
        parts = down(counts, place, tok, tie(ctx, far), mine, theirs)
        bits = [1 << i for i in range(size.bit_length() - 1)]
        swapped = swap(parts, bits.pop(0), size)
        near = shares(tie(where, parts), size - 3, 2, ctx, output_weight)

        q, ready = None, near
        for step in range(1, steps):
            got_up, got_down = lax.optimization_barrier((tie(ahead, ready), behind))
            if step < steps - 1:
                ahead = send(got_up, following, f"gather_up_{step + 1}")
                behind = send(got_down, preceding, f"gather_down_{step + 1}")
            else:
                ahead = send(got_up[:half], following, f"gather_up_{step + 1}")
                behind = send(got_down[half:], preceding, f"gather_down_{step + 1}")
            if step == 1:
                rest = shares(where, 0, size - 3, tie(ctx, got_up, got_down), output_weight)
                pieces, at_pieces, sofar = [tok, got_down, got_up], [0, 1, 2], []
            else:
                pieces, at_pieces, sofar = [got_down, got_up], [2 * step - 1, 2 * step], [q]
            q = add_products(tie(where, rest), pieces, at_pieces, query_weight, sofar)
            up_sum, down_sum, swapped = lax.optimization_barrier((tie(up_sum, q), down_sum, swapped))
            if swapped is not None:
                parts = meet(*swapped)
                swapped = None
            if bits:
                swapped = swap(tie(parts, up_sum), bits.pop(0), size)
            up_share, down_share = near[0], near[1]
            d = steps - step - 1
            near = rest[2 * d - 1], rest[2 * d]
            if step == 1:
                up_out = jnp.concatenate([up_share[:half] + widen(up_sum), up_share[half:]])
                down_out = jnp.concatenate([down_share[:half], down_share[half:] + widen(down_sum)])
            else:
                up_out, down_out = up_share + widen(up_sum), down_share + widen(down_sum)
            up_out, down_out = narrow(up_out), narrow(down_out)
            up_sum = send(up_out, following, f"scatter_up_{step + 1}")
            down_sum = send(down_out, preceding, f"scatter_down_{step + 1}")
            ready = (up_out, down_out)
        got_up, got_down, swapped = lax.optimization_barrier((tie(ahead, ready), behind, swapped))
        if swapped is not None:
            parts = meet(*swapped)
        for bit in bits:
            parts = meet(*swap(parts, bit, size))
        last = jnp.concatenate([got_up, got_down])
        up_q, up_o = up(counts, place, tie(parts, last), mine, theirs)
        q = add_products(where, [last], [size - 1], query_weight, [q, up_q], BF16)
        q_m = other_replica(q[packed - spare :])
        queries = unpack(counts, place, rows, (q, q_m))
        up_sum, down_sum = lax.optimization_barrier((tie(up_sum, queries), down_sum))
        o = (rest[0] + widen(up_sum) + widen(down_sum) + up_o).astype(BF16)
        o_m = other_replica(o[packed - spare :])
        attended = unpack(counts, place, rows, (o, o_m))
        return queries, attended

    return local


def solution(mesh):
    return jax.shard_map(
        make(mesh),
        mesh=mesh,
        in_specs=(
            P(("groups", "replica"), "tensor"),
            P(("groups", "replica"), "tensor"),
            P(None, "tensor"),
            P("tensor", None),
            P(("groups", "replica"), None, "tensor"),
            P(("groups", "replica"), None, "tensor"),
            P(("groups", "replica"), None, "tensor"),
            P(("groups", "replica"), None, "tensor"),
            P("groups"),
            P("groups"),
            P("groups"),
        ),
        out_specs=(P(("groups", "replica"), "tensor"), P(("groups", "replica"), "tensor")),
        check_vma=False,
    )
```

```python
import functools

import jax
import jax.numpy as jnp
from jax import lax
from jax.experimental import pallas as pl
from jax.experimental.pallas import tpu as pltpu
from jax.sharding import PartitionSpec as P

REQUEST_LENGTH = 256


adapter_scale = 0.5

SUM_SCALE = 8.0
DOWN_SCALE = 16.0

BF16 = jnp.bfloat16
F16 = jnp.float16
F32 = jnp.float32
I32 = jnp.int32

SMALL = 16 * 1024 * 1024
LARGE = 48 * 1024 * 1024
FULL = 62 * 1024 * 1024


def ring_order(size):
    if size == 8:
        return [0, 2, 4, 6, 7, 5, 3, 1]
    return list(range(size))


def send(value, pairs, name):
    with jax.named_scope(name):
        return lax.ppermute(value, "tensor", pairs)


def other_replica(value):
    return lax.ppermute(value, "replica", [(0, 1), (1, 0)])


def dot(a, b):
    return jnp.dot(a, b, preferred_element_type=F32)


def dot_t(a, b):
    return lax.dot_general(a, b, (((1,), (1,)), ((), ())), preferred_element_type=F32)


def look_up(index, table):
    out = I32(table[0])
    for i, entry in enumerate(table[1:], 1):
        out = jnp.where(index == i, I32(entry), out)
    return out


def whole(shape):
    return pl.BlockSpec(shape, lambda *_: (0,) * len(shape))


def params(limit=SMALL):
    return pltpu.CompilerParams(dimension_semantics=("arbitrary",), vmem_limit_bytes=limit)


def iota(shape, dim):
    return lax.broadcasted_iota(I32, shape, dim)


def lengths(counts, place):
    mine, theirs = 2 * place[0], 2 - 2 * place[0]
    return counts[mine], counts[mine + 1], counts[theirs], counts[theirs + 1]


def select_rows(home, x):
    hot = iota((home.shape[0], x.shape[0]), 1) == home
    return dot(hot.astype(F32).astype(BF16), x[...])


def home_of(position, live, c_a):
    home = jnp.where(position < c_a, position, REQUEST_LENGTH + position - c_a)
    return jnp.where(live, home, -1)


def spare_kernel(counts, place, x_ref, v_ref, out):
    spare = x_ref.shape[0]
    packed = 2 * REQUEST_LENGTH - spare
    c_a, c_b, d_a, d_b = lengths(counts, place)
    seat = iota((spare, 1), 0) + packed - spare - d_a - d_b
    home = home_of(packed + seat, seat >= 0, c_a) - packed
    out[:spare] = select_rows(home, x_ref).astype(BF16)
    out[spare:] = select_rows(home, v_ref).astype(BF16)


def spare_rows(counts, place, x, v, spare):
    shape = (2 * spare, x.shape[1])
    return pl.pallas_call(
        spare_kernel,
        grid_spec=pltpu.PrefetchScalarGridSpec(
            num_scalar_prefetch=2,
            grid=(1,),
            in_specs=[pl.BlockSpec((spare, x.shape[1]), lambda *_: (x.shape[0] // spare - 1, 0))] * 2,
            out_specs=whole(shape),
        ),
        out_shape=jax.ShapeDtypeStruct(shape, BF16),
        compiler_params=params(FULL),
        name="spare_rows",
    )(counts, place, x, v)


def pack_kernel(counts, place, x_ref, moved_ref, out):
    packed, spare = out.shape[0], moved_ref.shape[0]
    first = packed - spare
    c_a, c_b, _, _ = lengths(counts, place)
    slot = iota((packed, 1), 0)
    here = select_rows(home_of(slot, slot < c_a + c_b, c_a), x_ref)
    out[:first] = here[:first].astype(BF16)
    out[first:] = (here[first:] + moved_ref[...].astype(F32)).astype(BF16)


def pack(counts, place, x, moved, which):
    rows, width = x.shape
    spare = moved.shape[0] // 2
    shape = (rows - spare, width)
    return pl.pallas_call(
        pack_kernel,
        grid_spec=pltpu.PrefetchScalarGridSpec(
            num_scalar_prefetch=2,
            grid=(1,),
            in_specs=[whole(x.shape), pl.BlockSpec((spare, width), lambda *_: (which, 0))],
            out_specs=whole(shape),
        ),
        out_shape=jax.ShapeDtypeStruct(shape, BF16),
        compiler_params=params(LARGE),
        name="pack_rows",
    )(counts, place, x, moved)


def unpack_kernel(counts, place, x_ref, spare_ref, out):
    rows = out.shape[0]
    packed, spare = x_ref.shape[0], spare_ref.shape[0]
    first = packed - spare
    c_a, c_b, d_a, d_b = lengths(counts, place)
    n_theirs = d_a + d_b
    row = iota((rows, 1), 0)
    late = row >= REQUEST_LENGTH
    offset = jnp.where(late, row - REQUEST_LENGTH, row)
    position = offset + jnp.where(late, c_a, 0)
    target = jnp.where(position < packed, position, position + n_theirs - first)
    target = jnp.where(offset < jnp.where(late, c_b, c_a), target, -1)
    hot = (iota((rows, rows), 1) == target).astype(F32).astype(BF16)
    out[...] = (dot(hot[:, :packed], x_ref[...]) + dot(hot[:, packed:], spare_ref[...])).astype(BF16)


def unpack(counts, place, rows, parts):
    shape = (rows, parts[0].shape[1])
    return pl.pallas_call(
        unpack_kernel,
        grid_spec=pltpu.PrefetchScalarGridSpec(
            num_scalar_prefetch=2,
            grid=(1,),
            in_specs=[whole(p.shape) for p in parts],
            out_specs=whole(shape),
        ),
        out_shape=jax.ShapeDtypeStruct(shape, BF16),
        compiler_params=params(),
        name="unpack_rows",
    )(counts, place, *parts)


def request_of(counts, place, slot, packed):
    c_a, c_b, d_a, _ = lengths(counts, place)
    n_mine, replica = c_a + c_b, place[0]
    own = slot < n_mine
    seat = jnp.where(own, slot, packed + slot - n_mine)
    mine = 2 * replica + (seat >= c_a).astype(I32)
    theirs = 2 * (1 - replica) + (seat >= d_a).astype(I32)
    return jnp.where(own, mine, theirs)


def fetch_kernel(held, adapter_of, location, place, *refs):
    stores, out = refs[:4], refs[-1]
    slot = location[adapter_of[pl.program_id(0)]] - place[0] * held
    mine = (slot >= 0) & (slot < held)
    for k, table in enumerate(stores):
        block = table[0]
        out[k] = jnp.where(mine, block, jnp.zeros_like(block))


def fetch(stores, adapter_of, location, place, after):
    held, rank, width = stores[0].shape
    requests = adapter_of.shape[0]

    def at(i, adapter_of, location, place):
        slot = location[adapter_of[i]] - place[0] * held
        return jnp.clip(slot, 0, held - 1), 0, 0

    return pl.pallas_call(
        functools.partial(fetch_kernel, held),
        grid_spec=pltpu.PrefetchScalarGridSpec(
            num_scalar_prefetch=3,
            grid=(requests,),
            in_specs=[pl.BlockSpec((1, rank, width), at)] * 4 + [pl.BlockSpec(memory_space=pl.ANY)],
            out_specs=pl.BlockSpec((4, rank, width), lambda i, *_: (0, i, 0)),
        ),
        out_shape=jax.ShapeDtypeStruct((4, requests * rank, width), BF16),
        compiler_params=params(LARGE),
        name="fetch_blocks",
    )(adapter_of, location, place, *stores, after)


def down_kernel(counts, place, x, v, own, other, out, blocks):
    rank = out.shape[1] // 2
    packed, width = x.shape
    requests = own.shape[1] // rank
    blocks[...] = jnp.zeros_like(blocks)
    who = request_of(counts, place, iota((packed, 1), 0), packed)
    total = jnp.zeros(out.shape, F32)
    for i in range(requests):
        rows = pl.ds(i * rank, rank)
        blocks[:rank, :width] = own[0, rows] + other[0, rows]
        blocks[rank:, width:] = own[1, rows] + other[1, rows]
        got = dot_t(x[...], blocks[:, :width]) + dot_t(v[...], blocks[:, width:])
        total = total + jnp.where(who == i, got, 0.0)
    out[...] = total


def down(counts, place, x, v, own, other):
    requests_rank, width = own.shape[1:]
    rank = requests_rank // 4
    packed = x.shape[0]
    half = (2, requests_rank, width)
    return pl.pallas_call(
        down_kernel,
        grid_spec=pltpu.PrefetchScalarGridSpec(
            num_scalar_prefetch=2,
            grid=(1,),
            in_specs=[whole(v.shape) for v in (x, v)] + [whole(half)] * 2,
            out_specs=whole((packed, 2 * rank)),
            scratch_shapes=[pltpu.VMEM((2 * rank, 2 * width), BF16)],
        ),
        out_shape=jax.ShapeDtypeStruct((packed, 2 * rank), F32),
        compiler_params=params(),
        name="down_rows",
    )(counts, place, x, v, own, other)


def up_kernel(counts, place, low, own, other, q_ref, o_ref, blocks):
    packed, both = low.shape
    rank = both // 2
    width = q_ref.shape[1]
    requests = own.shape[1] // rank
    blocks[...] = jnp.zeros_like(blocks)
    who = request_of(counts, place, iota((packed, 1), 0), packed)
    rows_low = low[...].astype(BF16).astype(F32)
    for i in range(requests):
        rows = pl.ds(i * rank, rank)
        blocks[pl.ds(2 * i * rank, rank), :width] = own[0, rows] + other[0, rows]
        blocks[pl.ds((2 * i + 1) * rank, rank), width:] = own[1, rows] + other[1, rows]
    wide = jnp.concatenate(
        [jnp.where(who == i, rows_low, 0.0).astype(BF16) for i in range(requests)], axis=1
    )
    q_ref[...] = adapter_scale * dot(wide, blocks[:, :width])
    o_ref[...] = adapter_scale * dot(wide, blocks[:, width:])


def up(counts, place, low, own, other):
    packed, both = low.shape
    requests_rank, width = own.shape[1:]
    half = (2, requests_rank, width)
    return pl.pallas_call(
        up_kernel,
        grid_spec=pltpu.PrefetchScalarGridSpec(
            num_scalar_prefetch=2,
            grid=(1,),
            in_specs=[whole(low.shape)]
            + [pl.BlockSpec(half, lambda *_: (1, 0, 0))] * 2,
            out_specs=[whole((packed, width))] * 2,
            scratch_shapes=[pltpu.VMEM((2 * requests_rank, 2 * width), BF16)],
        ),
        out_shape=[jax.ShapeDtypeStruct((packed, width), F32)] * 2,
        compiler_params=params(),
        name="up_rows",
    )(counts, place, low, own, other)


def shares_kernel(where, x_ref, w_ref, out):
    out[0] = dot(x_ref[...], w_ref[...])


def shares(where, start, count, x, weight):
    rows, width = x.shape
    return pl.pallas_call(
        shares_kernel,
        grid_spec=pltpu.PrefetchScalarGridSpec(
            num_scalar_prefetch=1,
            grid=(count,),
            in_specs=[
                whole(x.shape),
                pl.BlockSpec((width, width), lambda i, where: (0, where[start + i])),
            ],
            out_specs=pl.BlockSpec((1, rows, width), lambda i, where: (i, 0, 0)),
        ),
        out_shape=jax.ShapeDtypeStruct((count, rows, width), F32),
        compiler_params=params(LARGE),
        name="shares",
    )(where, x, weight)


def add_kernel(pieces, where, *refs):
    xs, ws, extra, out = refs[:pieces], refs[pieces : 2 * pieces], refs[2 * pieces : -1], refs[-1]
    total = dot(xs[0][...], ws[0][...])
    for x, w in zip(xs[1:], ws[1:]):
        total = total + dot(x[...], w[...])
    for more in extra:
        total = total + more[...]
    out[...] = total.astype(out.dtype)


def add_products(where, pieces, at, weight, addends, dtype=F32):
    rows, width = pieces[0].shape
    columns = weight.shape[1]
    step = columns // 2

    def rows_of(i):
        return pl.BlockSpec((width, step), lambda j, where: (where[at[i]], j))

    tall = pl.BlockSpec((rows, step), lambda j, where: (0, j))
    return pl.pallas_call(
        functools.partial(add_kernel, len(pieces)),
        grid_spec=pltpu.PrefetchScalarGridSpec(
            num_scalar_prefetch=1,
            grid=(2,),
            in_specs=[whole(p.shape) for p in pieces]
            + [rows_of(i) for i in range(len(pieces))]
            + [tall] * len(addends),
            out_specs=tall,
        ),
        out_shape=jax.ShapeDtypeStruct((rows, columns), dtype),
        compiler_params=params(LARGE),
        name="add_products",
    )(where, *pieces, *([weight] * len(pieces)), *addends)


def narrow(value):
    return (value * SUM_SCALE).astype(F16)


def widen(value):
    return value.astype(F32) * (1.0 / SUM_SCALE)


def tie(value, *others):
    return lax.optimization_barrier((value, others))[0]


def swap(total, bit, size):
    mine = (total * DOWN_SCALE).astype(F16)
    return send(mine, [(t, t ^ bit) for t in range(size)], f"down_sums_{bit}"), mine


def meet(moved, mine):
    return (mine.astype(F32) + moved.astype(F32)) * (1.0 / DOWN_SCALE)


def make(mesh):
    size = mesh.shape["tensor"]
    order = ring_order(size)
    steps = size // 2
    following = [(order[p], order[(p + 1) % size]) for p in range(size)]
    preceding = [(b, a) for a, b in following]
    offsets = [0] + [sign * d for d in range(1, steps) for sign in (1, -1)] + [steps]
    place_of = [order.index(t) for t in range(size)]

    def local(
        tokens, context, query_weight, output_weight,
        store_aq, store_bq, store_ao, store_bo,
        adapter_of, location, token_count,
    ):
        rows, width = tokens.shape
        packed = rows * 3 // 4
        spare = rows - packed
        half = packed // 2
        at = lax.axis_index("tensor")
        place = jnp.stack([lax.axis_index("replica")]).astype(I32)
        counts = token_count
        where = jnp.stack(
            [look_up(at, [order[(p + d) % size] for p in place_of]) for d in offsets]
        )

        handed = spare_rows(counts, place, tokens, context, spare)
        moved = other_replica(handed)
        tok = pack(counts, place, tokens, moved, 0)
        ahead, behind = send(tok, following, "gather_up_1"), send(tok, preceding, "gather_down_1")
        ctx = pack(counts, tie(place, tok), context, moved, 1)
        farthest = shares(where, size - 1, 1, ctx, output_weight)
        far = narrow(farthest[0])
        up_sum = send(far[:half], following, "scatter_up_1")
        down_sum = send(far[half:], preceding, "scatter_down_1")
        stores = (store_aq, store_ao, store_bq, store_bo)
        mine = fetch(stores, adapter_of, location, place, tok)
        theirs = other_replica(mine)
        near = shares(tie(where, mine), size - 3, 2, ctx, output_weight)
        parts = down(counts, place, tok, tie(ctx, near), mine, theirs)
        bits = [1 << i for i in range(size.bit_length() - 1)]
        swapped = swap(parts, bits.pop(0), size)

        q, ready = None, parts
        for step in range(1, steps):
            got_up, got_down = lax.optimization_barrier((tie(ahead, ready), behind))
            if step < steps - 1:
                ahead = send(got_up, following, f"gather_up_{step + 1}")
                behind = send(got_down, preceding, f"gather_down_{step + 1}")
            else:
                ahead = send(got_up[:half], following, f"gather_up_{step + 1}")
                behind = send(got_down[half:], preceding, f"gather_down_{step + 1}")
            if step == 1:
                rest = shares(where, 0, size - 3, tie(ctx, got_up, got_down), output_weight)
                pieces, at_pieces, sofar = [tok, got_down, got_up], [0, 1, 2], []
            else:
                pieces, at_pieces, sofar = [got_down, got_up], [2 * step - 1, 2 * step], [q]
            q = add_products(tie(where, rest), pieces, at_pieces, query_weight, sofar)
            up_sum, down_sum, swapped = lax.optimization_barrier((tie(up_sum, q), down_sum, swapped))
            if swapped is not None:
                parts = meet(*swapped)
                swapped = None
            if bits:
                swapped = swap(tie(parts, up_sum), bits.pop(0), size)
            up_share, down_share = near[0], near[1]
            d = steps - step - 1
            near = rest[2 * d - 1], rest[2 * d]
            if step == 1:
                up_out = jnp.concatenate([up_share[:half] + widen(up_sum), up_share[half:]])
                down_out = jnp.concatenate([down_share[:half], down_share[half:] + widen(down_sum)])
            else:
                up_out, down_out = up_share + widen(up_sum), down_share + widen(down_sum)
            up_out, down_out = narrow(up_out), narrow(down_out)
            up_sum = send(up_out, following, f"scatter_up_{step + 1}")
            down_sum = send(down_out, preceding, f"scatter_down_{step + 1}")
            ready = (up_out, down_out)
        got_up, got_down, swapped = lax.optimization_barrier((tie(ahead, ready), behind, swapped))
        if swapped is not None:
            parts = meet(*swapped)
        for bit in bits:
            parts = meet(*swap(parts, bit, size))
        last = jnp.concatenate([got_up, got_down])
        up_q, up_o = up(counts, place, tie(parts, last), mine, theirs)
        q = add_products(where, [last], [size - 1], query_weight, [q, up_q], BF16)
        q_m = other_replica(q[packed - spare :])
        queries = unpack(counts, place, rows, (q, q_m))
        base = rest[0] + up_o
        up_sum, down_sum = lax.optimization_barrier((tie(up_sum, queries, base), down_sum))
        first = packed - spare
        o_last = (base[first:] + widen(up_sum[first:]) + widen(down_sum[first:])).astype(BF16)
        o_m = other_replica(o_last)
        o = (base + widen(up_sum) + widen(down_sum)).astype(BF16)
        attended = unpack(counts, place, rows, (o, o_m))
        return queries, attended

    return local


def solution(mesh):
    return jax.shard_map(
        make(mesh),
        mesh=mesh,
        in_specs=(
            P(("groups", "replica"), "tensor"),
            P(("groups", "replica"), "tensor"),
            P(None, "tensor"),
            P("tensor", None),
            P(("groups", "replica"), None, "tensor"),
            P(("groups", "replica"), None, "tensor"),
            P(("groups", "replica"), None, "tensor"),
            P(("groups", "replica"), None, "tensor"),
            P("groups"),
            P("groups"),
            P("groups"),
        ),
        out_specs=(P(("groups", "replica"), "tensor"), P(("groups", "replica"), "tensor")),
        check_vma=False,
    )
```

```python
import functools

import jax
import jax.numpy as jnp
from jax import lax
from jax.experimental import pallas as pl
from jax.experimental.pallas import tpu as pltpu
from jax.sharding import PartitionSpec as P

REQUEST_LENGTH = 256


adapter_scale = 0.5

SUM_SCALE = 8.0
DOWN_SCALE = 16.0

BF16 = jnp.bfloat16
F16 = jnp.float16
F32 = jnp.float32
I32 = jnp.int32

SMALL = 16 * 1024 * 1024
LARGE = 48 * 1024 * 1024
FULL = 62 * 1024 * 1024


def ring_order(size):
    if size == 8:
        return [0, 2, 4, 6, 7, 5, 3, 1]
    return list(range(size))


def send(value, pairs, name):
    with jax.named_scope(name):
        return lax.ppermute(value, "tensor", pairs)


def other_replica(value):
    return lax.ppermute(value, "replica", [(0, 1), (1, 0)])


def dot(a, b):
    return jnp.dot(a, b, preferred_element_type=F32)


def dot_t(a, b):
    return lax.dot_general(a, b, (((1,), (1,)), ((), ())), preferred_element_type=F32)


def look_up(index, table):
    out = I32(table[0])
    for i, entry in enumerate(table[1:], 1):
        out = jnp.where(index == i, I32(entry), out)
    return out


def whole(shape):
    return pl.BlockSpec(shape, lambda *_: (0,) * len(shape))


def params(limit=SMALL):
    return pltpu.CompilerParams(dimension_semantics=("arbitrary",), vmem_limit_bytes=limit)


def iota(shape, dim):
    return lax.broadcasted_iota(I32, shape, dim)


def lengths(counts, place):
    mine, theirs = 2 * place[0], 2 - 2 * place[0]
    return counts[mine], counts[mine + 1], counts[theirs], counts[theirs + 1]


def select_rows(home, x):
    hot = iota((home.shape[0], x.shape[0]), 1) == home
    return dot(hot.astype(F32).astype(BF16), x[...])


def home_of(position, live, c_a):
    home = jnp.where(position < c_a, position, REQUEST_LENGTH + position - c_a)
    return jnp.where(live, home, -1)


def spare_kernel(counts, place, x_ref, v_ref, out):
    spare = x_ref.shape[0]
    packed = 2 * REQUEST_LENGTH - spare
    c_a, c_b, d_a, d_b = lengths(counts, place)
    seat = iota((spare, 1), 0) + packed - spare - d_a - d_b
    home = home_of(packed + seat, seat >= 0, c_a) - packed
    out[:spare] = select_rows(home, x_ref).astype(BF16)
    out[spare:] = select_rows(home, v_ref).astype(BF16)


def spare_rows(counts, place, x, v, spare):
    shape = (2 * spare, x.shape[1])
    return pl.pallas_call(
        spare_kernel,
        grid_spec=pltpu.PrefetchScalarGridSpec(
            num_scalar_prefetch=2,
            grid=(1,),
            in_specs=[pl.BlockSpec((spare, x.shape[1]), lambda *_: (x.shape[0] // spare - 1, 0))] * 2,
            out_specs=whole(shape),
        ),
        out_shape=jax.ShapeDtypeStruct(shape, BF16),
        compiler_params=params(FULL),
        name="spare_rows",
    )(counts, place, x, v)


def pack_kernel(counts, place, x_ref, moved_ref, out):
    packed, spare = out.shape[0], moved_ref.shape[0]
    first = packed - spare
    c_a, c_b, _, _ = lengths(counts, place)
    slot = iota((packed, 1), 0)
    here = select_rows(home_of(slot, slot < c_a + c_b, c_a), x_ref)
    out[:first] = here[:first].astype(BF16)
    out[first:] = (here[first:] + moved_ref[...].astype(F32)).astype(BF16)


def pack(counts, place, x, moved, which):
    rows, width = x.shape
    spare = moved.shape[0] // 2
    shape = (rows - spare, width)
    return pl.pallas_call(
        pack_kernel,
        grid_spec=pltpu.PrefetchScalarGridSpec(
            num_scalar_prefetch=2,
            grid=(1,),
            in_specs=[whole(x.shape), pl.BlockSpec((spare, width), lambda *_: (which, 0))],
            out_specs=whole(shape),
        ),
        out_shape=jax.ShapeDtypeStruct(shape, BF16),
        compiler_params=params(LARGE),
        name="pack_rows",
    )(counts, place, x, moved)


def unpack_kernel(counts, place, x_ref, spare_ref, out):
    rows = out.shape[0]
    packed, spare = x_ref.shape[0], spare_ref.shape[0]
    first = packed - spare
    c_a, c_b, d_a, d_b = lengths(counts, place)
    n_theirs = d_a + d_b
    row = iota((rows, 1), 0)
    late = row >= REQUEST_LENGTH
    offset = jnp.where(late, row - REQUEST_LENGTH, row)
    position = offset + jnp.where(late, c_a, 0)
    target = jnp.where(position < packed, position, position + n_theirs - first)
    target = jnp.where(offset < jnp.where(late, c_b, c_a), target, -1)
    hot = (iota((rows, rows), 1) == target).astype(F32).astype(BF16)
    out[...] = (dot(hot[:, :packed], x_ref[...]) + dot(hot[:, packed:], spare_ref[...])).astype(BF16)


def unpack(counts, place, rows, parts):
    shape = (rows, parts[0].shape[1])
    return pl.pallas_call(
        unpack_kernel,
        grid_spec=pltpu.PrefetchScalarGridSpec(
            num_scalar_prefetch=2,
            grid=(1,),
            in_specs=[whole(p.shape) for p in parts],
            out_specs=whole(shape),
        ),
        out_shape=jax.ShapeDtypeStruct(shape, BF16),
        compiler_params=params(),
        name="unpack_rows",
    )(counts, place, *parts)


def request_of(counts, place, slot, packed):
    c_a, c_b, d_a, _ = lengths(counts, place)
    n_mine, replica = c_a + c_b, place[0]
    own = slot < n_mine
    seat = jnp.where(own, slot, packed + slot - n_mine)
    mine = 2 * replica + (seat >= c_a).astype(I32)
    theirs = 2 * (1 - replica) + (seat >= d_a).astype(I32)
    return jnp.where(own, mine, theirs)


def fetch_kernel(held, adapter_of, location, place, *refs):
    count = (len(refs) - 1) // 2
    stores, outs = refs[:count], refs[count + 1 :]
    slot = location[adapter_of[pl.program_id(0)]] - place[0] * held
    mine = (slot >= 0) & (slot < held)
    for table, out in zip(stores, outs):
        block = table[0]
        out[...] = jnp.where(mine, block, jnp.zeros_like(block))


def fetch(stores, adapter_of, location, place, after):
    held, rank, width = stores[0].shape
    requests = adapter_of.shape[0]

    def at(i, adapter_of, location, place):
        slot = location[adapter_of[i]] - place[0] * held
        return jnp.clip(slot, 0, held - 1), 0, 0

    return pl.pallas_call(
        functools.partial(fetch_kernel, held),
        grid_spec=pltpu.PrefetchScalarGridSpec(
            num_scalar_prefetch=3,
            grid=(requests,),
            in_specs=[pl.BlockSpec((1, rank, width), at)] * len(stores)
            + [pl.BlockSpec(memory_space=pl.ANY)],
            out_specs=[pl.BlockSpec((rank, width), lambda i, *_: (i, 0))] * len(stores),
        ),
        out_shape=[jax.ShapeDtypeStruct((requests * rank, width), BF16)] * len(stores),
        compiler_params=params(LARGE),
        name="fetch_blocks",
    )(adapter_of, location, place, *stores, after)


def down_kernel(counts, place, x, v, own_q, own_o, other_q, other_o, out, blocks):
    rank = out.shape[1] // 2
    packed, width = x.shape
    requests = own_q.shape[0] // rank
    blocks[...] = jnp.zeros_like(blocks)
    who = request_of(counts, place, iota((packed, 1), 0), packed)
    total = jnp.zeros(out.shape, F32)
    for i in range(requests):
        rows = pl.ds(i * rank, rank)
        blocks[:rank, :width] = own_q[rows] + other_q[rows]
        blocks[rank:, width:] = own_o[rows] + other_o[rows]
        got = dot_t(x[...], blocks[:, :width]) + dot_t(v[...], blocks[:, width:])
        total = total + jnp.where(who == i, got, 0.0)
    out[...] = total


def down(counts, place, x, v, own, other):
    requests_rank, width = own[0].shape
    rank = requests_rank // 4
    packed = x.shape[0]
    half = (requests_rank, width)
    return pl.pallas_call(
        down_kernel,
        grid_spec=pltpu.PrefetchScalarGridSpec(
            num_scalar_prefetch=2,
            grid=(1,),
            in_specs=[whole(v.shape) for v in (x, v)] + [whole(half)] * 4,
            out_specs=whole((packed, 2 * rank)),
            scratch_shapes=[pltpu.VMEM((2 * rank, 2 * width), BF16)],
        ),
        out_shape=jax.ShapeDtypeStruct((packed, 2 * rank), F32),
        compiler_params=params(),
        name="down_rows",
    )(counts, place, x, v, *own, *other)


def up_kernel(counts, place, low, own_q, own_o, other_q, other_o, q_ref, o_ref, blocks):
    packed, both = low.shape
    rank = both // 2
    width = q_ref.shape[1]
    requests = own_q.shape[0] // rank
    blocks[...] = jnp.zeros_like(blocks)
    who = request_of(counts, place, iota((packed, 1), 0), packed)
    rows_low = low[...].astype(BF16).astype(F32)
    for i in range(requests):
        rows = pl.ds(i * rank, rank)
        blocks[pl.ds(2 * i * rank, rank), :width] = own_q[rows] + other_q[rows]
        blocks[pl.ds((2 * i + 1) * rank, rank), width:] = own_o[rows] + other_o[rows]
    wide = jnp.concatenate(
        [jnp.where(who == i, rows_low, 0.0).astype(BF16) for i in range(requests)], axis=1
    )
    q_ref[...] = adapter_scale * dot(wide, blocks[:, :width])
    o_ref[...] = adapter_scale * dot(wide, blocks[:, width:])


def up(counts, place, low, own, other):
    packed, both = low.shape
    requests_rank, width = own[0].shape
    half = (requests_rank, width)
    return pl.pallas_call(
        up_kernel,
        grid_spec=pltpu.PrefetchScalarGridSpec(
            num_scalar_prefetch=2,
            grid=(1,),
            in_specs=[whole(low.shape)]
            + [whole(half)] * 4,
            out_specs=[whole((packed, width))] * 2,
            scratch_shapes=[pltpu.VMEM((2 * requests_rank, 2 * width), BF16)],
        ),
        out_shape=[jax.ShapeDtypeStruct((packed, width), F32)] * 2,
        compiler_params=params(),
        name="up_rows",
    )(counts, place, low, *own, *other)


def shares_kernel(where, x_ref, w_ref, out):
    out[0] = dot(x_ref[...], w_ref[...])


def shares(where, start, count, x, weight):
    rows, width = x.shape
    return pl.pallas_call(
        shares_kernel,
        grid_spec=pltpu.PrefetchScalarGridSpec(
            num_scalar_prefetch=1,
            grid=(count,),
            in_specs=[
                whole(x.shape),
                pl.BlockSpec((width, width), lambda i, where: (0, where[start + i])),
            ],
            out_specs=pl.BlockSpec((1, rows, width), lambda i, where: (i, 0, 0)),
        ),
        out_shape=jax.ShapeDtypeStruct((count, rows, width), F32),
        compiler_params=params(LARGE),
        name="shares",
    )(where, x, weight)


def add_kernel(pieces, where, *refs):
    xs, ws, extra, out = refs[:pieces], refs[pieces : 2 * pieces], refs[2 * pieces : -1], refs[-1]
    total = dot(xs[0][...], ws[0][...])
    for x, w in zip(xs[1:], ws[1:]):
        total = total + dot(x[...], w[...])
    for more in extra:
        total = total + more[...]
    out[...] = total.astype(out.dtype)


def add_products(where, pieces, at, weight, addends, dtype=F32):
    rows, width = pieces[0].shape
    columns = weight.shape[1]
    step = columns // 2

    def rows_of(i):
        return pl.BlockSpec((width, step), lambda j, where: (where[at[i]], j))

    tall = pl.BlockSpec((rows, step), lambda j, where: (0, j))
    return pl.pallas_call(
        functools.partial(add_kernel, len(pieces)),
        grid_spec=pltpu.PrefetchScalarGridSpec(
            num_scalar_prefetch=1,
            grid=(2,),
            in_specs=[whole(p.shape) for p in pieces]
            + [rows_of(i) for i in range(len(pieces))]
            + [tall] * len(addends),
            out_specs=tall,
        ),
        out_shape=jax.ShapeDtypeStruct((rows, columns), dtype),
        compiler_params=params(LARGE),
        name="add_products",
    )(where, *pieces, *([weight] * len(pieces)), *addends)


def narrow(value):
    return (value * SUM_SCALE).astype(F16)


def widen(value):
    return value.astype(F32) * (1.0 / SUM_SCALE)


def tie(value, *others):
    return lax.optimization_barrier((value, others))[0]


def swap(total, bit, size):
    mine = (total * DOWN_SCALE).astype(F16)
    return send(mine, [(t, t ^ bit) for t in range(size)], f"down_sums_{bit}"), mine


def meet(moved, mine):
    return (mine.astype(F32) + moved.astype(F32)) * (1.0 / DOWN_SCALE)


def make(mesh):
    size = mesh.shape["tensor"]
    order = ring_order(size)
    steps = size // 2
    following = [(order[p], order[(p + 1) % size]) for p in range(size)]
    preceding = [(b, a) for a, b in following]
    offsets = [0] + [sign * d for d in range(1, steps) for sign in (1, -1)] + [steps]
    place_of = [order.index(t) for t in range(size)]

    def local(
        tokens, context, query_weight, output_weight,
        store_aq, store_bq, store_ao, store_bo,
        adapter_of, location, token_count,
    ):
        rows, width = tokens.shape
        packed = rows * 3 // 4
        spare = rows - packed
        half = packed // 2
        at = lax.axis_index("tensor")
        place = jnp.stack([lax.axis_index("replica")]).astype(I32)
        counts = token_count
        where = jnp.stack(
            [look_up(at, [order[(p + d) % size] for p in place_of]) for d in offsets]
        )

        handed = spare_rows(counts, place, tokens, context, spare)
        moved = other_replica(handed)
        tok = pack(counts, place, tokens, moved, 0)
        ahead, behind = send(tok, following, "gather_up_1"), send(tok, preceding, "gather_down_1")
        ctx = pack(counts, tie(place, tok), context, moved, 1)
        farthest = shares(where, size - 1, 1, ctx, output_weight)
        far = narrow(farthest[0])
        up_sum = send(far[:half], following, "scatter_up_1")
        down_sum = send(far[half:], preceding, "scatter_down_1")
        mine = fetch((store_aq, store_ao), adapter_of, location, place, tok)
        theirs = [other_replica(blocks) for blocks in mine]
        near = shares(tie(where, mine), size - 3, 2, ctx, output_weight)
        parts = down(counts, place, tok, tie(ctx, near), mine, theirs)
        bits = [1 << i for i in range(size.bit_length() - 1)]
        swapped = swap(parts, bits.pop(0), size)

        q, ready = None, parts
        for step in range(1, steps):
            got_up, got_down = lax.optimization_barrier((tie(ahead, ready), behind))
            if step < steps - 1:
                ahead = send(got_up, following, f"gather_up_{step + 1}")
                behind = send(got_down, preceding, f"gather_down_{step + 1}")
            else:
                up_half, down_half = lax.optimization_barrier((got_up[:half], got_down[half:]))
                ahead = send(up_half, following, f"gather_up_{step + 1}")
                behind = send(down_half, preceding, f"gather_down_{step + 1}")
                rest = tie(rest, up_half, down_half)
            if step == 1:
                rest = shares(where, 0, size - 3, tie(ctx, got_up, got_down), output_weight)
                pieces, at_pieces, sofar = [tok, got_down, got_up], [0, 1, 2], []
            else:
                pieces, at_pieces, sofar = [got_down, got_up], [2 * step - 1, 2 * step], [q]
            q = add_products(tie(where, rest), pieces, at_pieces, query_weight, sofar)
            if step == 2:
                mine = fetch((store_bq, store_bo), adapter_of, location, place, q)
            up_sum, down_sum, swapped = lax.optimization_barrier((tie(up_sum, q), down_sum, swapped))
            if swapped is not None:
                parts = meet(*swapped)
                swapped = None
            if bits:
                swapped = swap(tie(parts, up_sum), bits.pop(0), size)
            up_share, down_share = near[0], near[1]
            d = steps - step - 1
            near = rest[2 * d - 1], rest[2 * d]
            if step == 1:
                up_out = jnp.concatenate([up_share[:half] + widen(up_sum), up_share[half:]])
                down_out = jnp.concatenate([down_share[:half], down_share[half:] + widen(down_sum)])
            else:
                up_out, down_out = up_share + widen(up_sum), down_share + widen(down_sum)
            up_out, down_out = narrow(up_out), narrow(down_out)
            up_sum = send(up_out, following, f"scatter_up_{step + 1}")
            down_sum = send(down_out, preceding, f"scatter_down_{step + 1}")
            ready = (up_out, down_out)
        theirs = [other_replica(tie(blocks, up_out, down_out)) for blocks in mine]
        got_up, got_down, swapped = lax.optimization_barrier((tie(ahead, ready), behind, swapped))
        if swapped is not None:
            parts = meet(*swapped)
        for bit in bits:
            parts = meet(*swap(parts, bit, size))
        last = jnp.concatenate([got_up, got_down])
        up_q, up_o = up(counts, place, tie(parts, last), mine, theirs)
        q = add_products(where, [last], [size - 1], query_weight, [q, up_q], BF16)
        q_m = other_replica(q[packed - spare :])
        queries = unpack(counts, place, rows, (q, q_m))
        base = rest[0] + up_o
        up_sum, down_sum = lax.optimization_barrier((tie(up_sum, queries, base), down_sum))
        first = packed - spare
        o_last = (base[first:] + widen(up_sum[first:]) + widen(down_sum[first:])).astype(BF16)
        o_m = other_replica(o_last)
        o = (base + widen(up_sum) + widen(down_sum)).astype(BF16)
        attended = unpack(counts, place, rows, (o, o_m))
        return queries, attended

    return local


def solution(mesh):
    return jax.shard_map(
        make(mesh),
        mesh=mesh,
        in_specs=(
            P(("groups", "replica"), "tensor"),
            P(("groups", "replica"), "tensor"),
            P(None, "tensor"),
            P("tensor", None),
            P(("groups", "replica"), None, "tensor"),
            P(("groups", "replica"), None, "tensor"),
            P(("groups", "replica"), None, "tensor"),
            P(("groups", "replica"), None, "tensor"),
            P("groups"),
            P("groups"),
            P("groups"),
        ),
        out_specs=(P(("groups", "replica"), "tensor"), P(("groups", "replica"), "tensor")),
        check_vma=False,
    )
```

```python
import functools

import jax
import jax.numpy as jnp
from jax import lax
from jax.experimental import pallas as pl
from jax.experimental.pallas import tpu as pltpu
from jax.sharding import PartitionSpec as P

REQUEST_LENGTH = 256


adapter_scale = 0.5

SUM_SCALE = 8.0
DOWN_SCALE = 16.0

BF16 = jnp.bfloat16
F16 = jnp.float16
F32 = jnp.float32
I32 = jnp.int32

SMALL = 16 * 1024 * 1024
LARGE = 40 * 1024 * 1024
FULL = 62 * 1024 * 1024


def ring_order(size):
    if size == 8:
        return [0, 2, 4, 6, 7, 5, 3, 1]
    return list(range(size))


def send(value, pairs, name):
    with jax.named_scope(name):
        return lax.ppermute(value, "tensor", pairs)


def other_replica(value):
    return lax.ppermute(value, "replica", [(0, 1), (1, 0)])


def dot(a, b):
    return jnp.dot(a, b, preferred_element_type=F32)


def dot_t(a, b):
    return lax.dot_general(a, b, (((1,), (1,)), ((), ())), preferred_element_type=F32)


def look_up(index, table):
    out = I32(table[0])
    for i, entry in enumerate(table[1:], 1):
        out = jnp.where(index == i, I32(entry), out)
    return out


def whole(shape):
    return pl.BlockSpec(shape, lambda *_: (0,) * len(shape))


def params(limit=SMALL):
    return pltpu.CompilerParams(dimension_semantics=("arbitrary",), vmem_limit_bytes=limit)


def iota(shape, dim):
    return lax.broadcasted_iota(I32, shape, dim)


def lengths(counts, place):
    mine, theirs = 2 * place[0], 2 - 2 * place[0]
    return counts[mine], counts[mine + 1], counts[theirs], counts[theirs + 1]


def select_rows(home, x):
    hot = iota((home.shape[0], x.shape[0]), 1) == home
    return dot(hot.astype(F32).astype(BF16), x[...])


def home_of(position, live, c_a):
    home = jnp.where(position < c_a, position, REQUEST_LENGTH + position - c_a)
    return jnp.where(live, home, -1)


def pack_kernel(counts, place, x_ref, out):
    c_a, c_b, _, _ = lengths(counts, place)
    slot = iota((out.shape[0], 1), 0)
    out[...] = select_rows(home_of(slot, slot < c_a + c_b, c_a), x_ref).astype(BF16)


def pack(counts, place, x):
    rows, width = x.shape
    shape = (rows * 3 // 4, width)
    return pl.pallas_call(
        pack_kernel,
        grid_spec=pltpu.PrefetchScalarGridSpec(
            num_scalar_prefetch=2,
            grid=(1,),
            in_specs=[whole(x.shape)],
            out_specs=whole(shape),
        ),
        out_shape=jax.ShapeDtypeStruct(shape, BF16),
        compiler_params=params(LARGE),
        name="pack_rows",
    )(counts, place, x)


def fill_kernel(packed, counts, place, x_ref, theirs_ref, out):
    spare = out.shape[0]
    c_a, c_b, d_a, _ = lengths(counts, place)
    n_mine = c_a + c_b
    slot = iota((spare, 1), 0) + packed - spare
    home = packed + slot - n_mine - d_a + REQUEST_LENGTH - (2 * REQUEST_LENGTH - spare)
    there = select_rows(jnp.where(slot < n_mine, -1, home), theirs_ref)
    out[...] = (x_ref[...].astype(F32) + there).astype(BF16)


def fill(counts, place, x, theirs):
    packed, width = x.shape
    rows = theirs.shape[0]
    spare = rows - packed
    last = pl.BlockSpec((spare, width), lambda *_: (packed // spare - 1, 0))
    return pl.pallas_call(
        functools.partial(fill_kernel, packed),
        grid_spec=pltpu.PrefetchScalarGridSpec(
            num_scalar_prefetch=2,
            grid=(1,),
            in_specs=[last, pl.BlockSpec((spare, width), lambda *_: (rows // spare - 1, 0))],
            out_specs=last,
        ),
        out_shape=jax.ShapeDtypeStruct(x.shape, BF16),
        input_output_aliases={2: 0},
        compiler_params=params(LARGE),
        name="fill_rows",
    )(counts, place, x, theirs)


def unpack_kernel(counts, place, x_ref, spare_ref, out):
    rows = out.shape[0]
    packed, spare = x_ref.shape[0], spare_ref.shape[0]
    first = packed - spare
    c_a, c_b, d_a, d_b = lengths(counts, place)
    n_theirs = d_a + d_b
    row = iota((rows, 1), 0)
    late = row >= REQUEST_LENGTH
    offset = jnp.where(late, row - REQUEST_LENGTH, row)
    position = offset + jnp.where(late, c_a, 0)
    target = jnp.where(position < packed, position, position + n_theirs - first)
    target = jnp.where(offset < jnp.where(late, c_b, c_a), target, -1)
    hot = (iota((rows, rows), 1) == target).astype(F32).astype(BF16)
    out[...] = (dot(hot[:, :packed], x_ref[...]) + dot(hot[:, packed:], spare_ref[...])).astype(BF16)


def unpack(counts, place, rows, parts):
    shape = (rows, parts[0].shape[1])
    return pl.pallas_call(
        unpack_kernel,
        grid_spec=pltpu.PrefetchScalarGridSpec(
            num_scalar_prefetch=2,
            grid=(1,),
            in_specs=[whole(p.shape) for p in parts],
            out_specs=whole(shape),
        ),
        out_shape=jax.ShapeDtypeStruct(shape, BF16),
        compiler_params=params(),
        name="unpack_rows",
    )(counts, place, *parts)


def request_of(counts, place, slot, packed):
    c_a, c_b, d_a, _ = lengths(counts, place)
    n_mine, replica = c_a + c_b, place[0]
    own = slot < n_mine
    seat = jnp.where(own, slot, packed + slot - n_mine)
    mine = 2 * replica + (seat >= c_a).astype(I32)
    theirs = 2 * (1 - replica) + (seat >= d_a).astype(I32)
    return jnp.where(own, mine, theirs)


def fetch_kernel(held, adapter_of, location, place, *refs):
    count = (len(refs) - 1) // 2
    stores, outs = refs[:count], refs[count + 1 :]
    slot = location[adapter_of[pl.program_id(0)]] - place[0] * held
    mine = (slot >= 0) & (slot < held)
    for table, out in zip(stores, outs):
        block = table[0]
        out[...] = jnp.where(mine, block, jnp.zeros_like(block))


def fetch(stores, adapter_of, location, place, after):
    held, rank, width = stores[0].shape
    requests = adapter_of.shape[0]

    def at(i, adapter_of, location, place):
        slot = location[adapter_of[i]] - place[0] * held
        return jnp.clip(slot, 0, held - 1), 0, 0

    return pl.pallas_call(
        functools.partial(fetch_kernel, held),
        grid_spec=pltpu.PrefetchScalarGridSpec(
            num_scalar_prefetch=3,
            grid=(requests,),
            in_specs=[pl.BlockSpec((1, rank, width), at)] * len(stores)
            + [pl.BlockSpec(memory_space=pl.ANY)],
            out_specs=[pl.BlockSpec((rank, width), lambda i, *_: (i, 0))] * len(stores),
        ),
        out_shape=[jax.ShapeDtypeStruct((requests * rank, width), BF16)] * len(stores),
        compiler_params=params(LARGE),
        name="fetch_blocks",
    )(adapter_of, location, place, *stores, after)


def down_kernel(counts, place, x, v, own_q, own_o, other_q, other_o, out, blocks):
    rank = out.shape[1] // 2
    packed, width = x.shape
    requests = own_q.shape[0] // rank
    blocks[...] = jnp.zeros_like(blocks)
    who = request_of(counts, place, iota((packed, 1), 0), packed)
    total = jnp.zeros(out.shape, F32)
    for i in range(requests):
        rows = pl.ds(i * rank, rank)
        blocks[:rank, :width] = own_q[rows] + other_q[rows]
        blocks[rank:, width:] = own_o[rows] + other_o[rows]
        got = dot_t(x[...], blocks[:, :width]) + dot_t(v[...], blocks[:, width:])
        total = total + jnp.where(who == i, got, 0.0)
    out[...] = total


def down(counts, place, x, v, own, other):
    requests_rank, width = own[0].shape
    rank = requests_rank // 4
    packed = x.shape[0]
    half = (requests_rank, width)
    return pl.pallas_call(
        down_kernel,
        grid_spec=pltpu.PrefetchScalarGridSpec(
            num_scalar_prefetch=2,
            grid=(1,),
            in_specs=[whole(v.shape) for v in (x, v)] + [whole(half)] * 4,
            out_specs=whole((packed, 2 * rank)),
            scratch_shapes=[pltpu.VMEM((2 * rank, 2 * width), BF16)],
        ),
        out_shape=jax.ShapeDtypeStruct((packed, 2 * rank), F32),
        compiler_params=params(),
        name="down_rows",
    )(counts, place, x, v, *own, *other)


def up_kernel(counts, place, low, own_q, own_o, other_q, other_o, q_ref, o_ref, blocks):
    packed, both = low.shape
    rank = both // 2
    width = q_ref.shape[1]
    requests = own_q.shape[0] // rank
    blocks[...] = jnp.zeros_like(blocks)
    who = request_of(counts, place, iota((packed, 1), 0), packed)
    rows_low = low[...].astype(BF16).astype(F32)
    for i in range(requests):
        rows = pl.ds(i * rank, rank)
        blocks[pl.ds(2 * i * rank, rank), :width] = own_q[rows] + other_q[rows]
        blocks[pl.ds((2 * i + 1) * rank, rank), width:] = own_o[rows] + other_o[rows]
    wide = jnp.concatenate(
        [jnp.where(who == i, rows_low, 0.0).astype(BF16) for i in range(requests)], axis=1
    )
    q_ref[...] = adapter_scale * dot(wide, blocks[:, :width])
    o_ref[...] = adapter_scale * dot(wide, blocks[:, width:])


def up(counts, place, low, own, other):
    packed, both = low.shape
    requests_rank, width = own[0].shape
    half = (requests_rank, width)
    return pl.pallas_call(
        up_kernel,
        grid_spec=pltpu.PrefetchScalarGridSpec(
            num_scalar_prefetch=2,
            grid=(1,),
            in_specs=[whole(low.shape)]
            + [whole(half)] * 4,
            out_specs=[whole((packed, width))] * 2,
            scratch_shapes=[pltpu.VMEM((2 * requests_rank, 2 * width), BF16)],
        ),
        out_shape=[jax.ShapeDtypeStruct((packed, width), F32)] * 2,
        compiler_params=params(),
        name="up_rows",
    )(counts, place, low, *own, *other)


def shares_kernel(where, x_ref, w_ref, out):
    out[0] = dot(x_ref[...], w_ref[...])


def shares(where, start, count, x, weight):
    rows, width = x.shape
    return pl.pallas_call(
        shares_kernel,
        grid_spec=pltpu.PrefetchScalarGridSpec(
            num_scalar_prefetch=1,
            grid=(count,),
            in_specs=[
                whole(x.shape),
                pl.BlockSpec((width, width), lambda i, where: (0, where[start + i])),
            ],
            out_specs=pl.BlockSpec((1, rows, width), lambda i, where: (i, 0, 0)),
        ),
        out_shape=jax.ShapeDtypeStruct((count, rows, width), F32),
        compiler_params=params(LARGE),
        name="shares",
    )(where, x, weight)


def add_kernel(pieces, where, *refs):
    xs, ws, extra, out = refs[:pieces], refs[pieces : 2 * pieces], refs[2 * pieces : -1], refs[-1]
    total = dot(xs[0][...], ws[0][...])
    for x, w in zip(xs[1:], ws[1:]):
        total = total + dot(x[...], w[...])
    for more in extra:
        total = total + more[...]
    out[...] = total.astype(out.dtype)


def add_products(where, pieces, at, weight, addends, dtype=F32):
    rows, width = pieces[0].shape
    columns = weight.shape[1]
    step = columns // 2

    def rows_of(i):
        return pl.BlockSpec((width, step), lambda j, where: (where[at[i]], j))

    tall = pl.BlockSpec((rows, step), lambda j, where: (0, j))
    return pl.pallas_call(
        functools.partial(add_kernel, len(pieces)),
        grid_spec=pltpu.PrefetchScalarGridSpec(
            num_scalar_prefetch=1,
            grid=(2,),
            in_specs=[whole(p.shape) for p in pieces]
            + [rows_of(i) for i in range(len(pieces))]
            + [tall] * len(addends),
            out_specs=tall,
        ),
        out_shape=jax.ShapeDtypeStruct((rows, columns), dtype),
        compiler_params=params(LARGE),
        name="add_products",
    )(where, *pieces, *([weight] * len(pieces)), *addends)


def narrow(value):
    return (value * SUM_SCALE).astype(F16)


def widen(value):
    return value.astype(F32) * (1.0 / SUM_SCALE)


def tie(value, *others):
    return lax.optimization_barrier((value, others))[0]


def swap(total, bit, size):
    mine = (total * DOWN_SCALE).astype(F16)
    return send(mine, [(t, t ^ bit) for t in range(size)], f"down_sums_{bit}"), mine


def meet(moved, mine):
    return (mine.astype(F32) + moved.astype(F32)) * (1.0 / DOWN_SCALE)


def make(mesh):
    size = mesh.shape["tensor"]
    order = ring_order(size)
    steps = size // 2
    following = [(order[p], order[(p + 1) % size]) for p in range(size)]
    preceding = [(b, a) for a, b in following]
    offsets = [0] + [sign * d for d in range(1, steps) for sign in (1, -1)] + [steps]
    place_of = [order.index(t) for t in range(size)]

    def local(
        tokens, context, query_weight, output_weight,
        store_aq, store_bq, store_ao, store_bo,
        adapter_of, location, token_count,
    ):
        rows, width = tokens.shape
        packed = rows * 3 // 4
        spare = rows - packed
        half = packed // 2
        at = lax.axis_index("tensor")
        place = jnp.stack([lax.axis_index("replica")]).astype(I32)
        counts = token_count
        where = jnp.stack(
            [look_up(at, [order[(p + d) % size] for p in place_of]) for d in offsets]
        )

        tok = fill(counts, place, pack(counts, place, tokens), other_replica(tokens))
        ahead, behind = send(tok, following, "gather_up_1"), send(tok, preceding, "gather_down_1")
        ctx = fill(counts, tie(place, tok), pack(counts, tie(place, tok), context), other_replica(context))
        farthest = shares(where, size - 1, 1, ctx, output_weight)
        far = narrow(farthest[0])
        up_sum = send(far[:half], following, "scatter_up_1")
        down_sum = send(far[half:], preceding, "scatter_down_1")
        mine = fetch((store_aq, store_ao), adapter_of, location, place, tok)
        theirs = [other_replica(blocks) for blocks in mine]
        near = shares(tie(where, mine), size - 3, 2, ctx, output_weight)
        parts = down(counts, place, tok, tie(ctx, near), mine, theirs)
        bits = [1 << i for i in range(size.bit_length() - 1)]
        swapped = swap(parts, bits.pop(0), size)

        q, ready = None, parts
        for step in range(1, steps):
            got_up, got_down = lax.optimization_barrier((tie(ahead, ready), behind))
            if step < steps - 1:
                ahead = send(got_up, following, f"gather_up_{step + 1}")
                behind = send(got_down, preceding, f"gather_down_{step + 1}")
            else:
                up_half, down_half = lax.optimization_barrier((got_up[:half], got_down[half:]))
                ahead = send(up_half, following, f"gather_up_{step + 1}")
                behind = send(down_half, preceding, f"gather_down_{step + 1}")
                rest = tie(rest, up_half, down_half)
            if step == 1:
                rest = shares(where, 0, size - 3, tie(ctx, got_up, got_down), output_weight)
                pieces, at_pieces, sofar = [tok, got_down, got_up], [0, 1, 2], []
            else:
                pieces, at_pieces, sofar = [got_down, got_up], [2 * step - 1, 2 * step], [q]
            q = add_products(tie(where, rest), pieces, at_pieces, query_weight, sofar)
            if step == 2:
                mine = fetch((store_bq, store_bo), adapter_of, location, place, q)
            up_sum, down_sum, swapped = lax.optimization_barrier((tie(up_sum, q), down_sum, swapped))
            if swapped is not None:
                parts = meet(*swapped)
                swapped = None
            if bits:
                swapped = swap(tie(parts, up_sum), bits.pop(0), size)
            up_share, down_share = near[0], near[1]
            d = steps - step - 1
            near = rest[2 * d - 1], rest[2 * d]
            if step == 1:
                up_out = jnp.concatenate([up_share[:half] + widen(up_sum), up_share[half:]])
                down_out = jnp.concatenate([down_share[:half], down_share[half:] + widen(down_sum)])
            else:
                up_out, down_out = up_share + widen(up_sum), down_share + widen(down_sum)
            up_out, down_out = narrow(up_out), narrow(down_out)
            up_sum = send(up_out, following, f"scatter_up_{step + 1}")
            down_sum = send(down_out, preceding, f"scatter_down_{step + 1}")
            ready = (up_out, down_out)
        theirs = [other_replica(tie(blocks, up_out, down_out)) for blocks in mine]
        got_up, got_down, swapped = lax.optimization_barrier((tie(ahead, ready), behind, swapped))
        if swapped is not None:
            parts = meet(*swapped)
        for bit in bits:
            parts = meet(*swap(parts, bit, size))
        last = jnp.concatenate([got_up, got_down])
        up_q, up_o = up(counts, place, tie(parts, last), mine, theirs)
        q = add_products(where, [last], [size - 1], query_weight, [q, up_q], BF16)
        q_m = other_replica(q[packed - spare :])
        queries = unpack(counts, place, rows, (q, q_m))
        base = rest[0] + up_o
        up_sum, down_sum = lax.optimization_barrier((tie(up_sum, queries, base), down_sum))
        first = packed - spare
        o_last = (base[first:] + widen(up_sum[first:]) + widen(down_sum[first:])).astype(BF16)
        o_m = other_replica(o_last)
        o = (base + widen(up_sum) + widen(down_sum)).astype(BF16)
        attended = unpack(counts, place, rows, (o, o_m))
        return queries, attended

    return local


def solution(mesh):
    return jax.shard_map(
        make(mesh),
        mesh=mesh,
        in_specs=(
            P(("groups", "replica"), "tensor"),
            P(("groups", "replica"), "tensor"),
            P(None, "tensor"),
            P("tensor", None),
            P(("groups", "replica"), None, "tensor"),
            P(("groups", "replica"), None, "tensor"),
            P(("groups", "replica"), None, "tensor"),
            P(("groups", "replica"), None, "tensor"),
            P("groups"),
            P("groups"),
            P("groups"),
        ),
        out_specs=(P(("groups", "replica"), "tensor"), P(("groups", "replica"), "tensor")),
        check_vma=False,
    )
```

```python
import functools

import jax
import jax.numpy as jnp
from jax import lax
from jax.experimental import pallas as pl
from jax.experimental.pallas import tpu as pltpu
from jax.sharding import PartitionSpec as P

REQUEST_LENGTH = 256


adapter_scale = 0.5

SUM_SCALE = 8.0
DOWN_SCALE = 16.0

BF16 = jnp.bfloat16
F16 = jnp.float16
F32 = jnp.float32
I32 = jnp.int32

SMALL = 16 * 1024 * 1024
LARGE = 40 * 1024 * 1024
FULL = 62 * 1024 * 1024


def ring_order(size):
    if size == 8:
        return [0, 2, 4, 6, 7, 5, 3, 1]
    return list(range(size))


def send(value, pairs, name):
    with jax.named_scope(name):
        return lax.ppermute(value, "tensor", pairs)


def other_replica(value):
    return lax.ppermute(value, "replica", [(0, 1), (1, 0)])


def dot(a, b):
    return jnp.dot(a, b, preferred_element_type=F32)


def dot_t(a, b):
    return lax.dot_general(a, b, (((1,), (1,)), ((), ())), preferred_element_type=F32)


def look_up(index, table):
    out = I32(table[0])
    for i, entry in enumerate(table[1:], 1):
        out = jnp.where(index == i, I32(entry), out)
    return out


def whole(shape):
    return pl.BlockSpec(shape, lambda *_: (0,) * len(shape))


def params(limit=SMALL):
    return pltpu.CompilerParams(dimension_semantics=("arbitrary",), vmem_limit_bytes=limit)


def iota(shape, dim):
    return lax.broadcasted_iota(I32, shape, dim)


def lengths(counts, place):
    mine, theirs = 2 * place[0], 2 - 2 * place[0]
    return counts[mine], counts[mine + 1], counts[theirs], counts[theirs + 1]


def select_rows(home, x):
    hot = iota((home.shape[0], x.shape[0]), 1) == home
    return dot(hot.astype(F32).astype(BF16), x[...])


def home_of(position, live, c_a):
    home = jnp.where(position < c_a, position, REQUEST_LENGTH + position - c_a)
    return jnp.where(live, home, -1)


def pack_kernel(counts, place, x_ref, out):
    c_a, c_b, _, _ = lengths(counts, place)
    slot = iota((out.shape[0], 1), 0)
    out[...] = select_rows(home_of(slot, slot < c_a + c_b, c_a), x_ref).astype(BF16)


def pack(counts, place, x):
    rows, width = x.shape
    shape = (rows * 3 // 4, width)
    return pl.pallas_call(
        pack_kernel,
        grid_spec=pltpu.PrefetchScalarGridSpec(
            num_scalar_prefetch=2,
            grid=(1,),
            in_specs=[whole(x.shape)],
            out_specs=whole(shape),
        ),
        out_shape=jax.ShapeDtypeStruct(shape, BF16),
        compiler_params=params(LARGE),
        name="pack_rows",
    )(counts, place, x)


def fill_kernel(packed, counts, place, x_ref, theirs_ref, out):
    spare = out.shape[0]
    c_a, c_b, d_a, _ = lengths(counts, place)
    n_mine = c_a + c_b
    slot = iota((spare, 1), 0) + packed - spare
    home = packed + slot - n_mine - d_a + REQUEST_LENGTH - (2 * REQUEST_LENGTH - spare)
    there = select_rows(jnp.where(slot < n_mine, -1, home), theirs_ref)
    out[...] = (x_ref[...].astype(F32) + there).astype(BF16)


def fill(counts, place, x, theirs):
    packed, width = x.shape
    rows = theirs.shape[0]
    spare = rows - packed
    last = pl.BlockSpec((spare, width), lambda *_: (packed // spare - 1, 0))
    return pl.pallas_call(
        functools.partial(fill_kernel, packed),
        grid_spec=pltpu.PrefetchScalarGridSpec(
            num_scalar_prefetch=2,
            grid=(1,),
            in_specs=[last, pl.BlockSpec((spare, width), lambda *_: (rows // spare - 1, 0))],
            out_specs=last,
        ),
        out_shape=jax.ShapeDtypeStruct(x.shape, BF16),
        input_output_aliases={2: 0},
        compiler_params=params(LARGE),
        name="fill_rows",
    )(counts, place, x, theirs)


def seats_kernel(packed, counts, place, out):
    rows = out.shape[0]
    first = 2 * packed - rows
    c_a, c_b, d_a, d_b = lengths(counts, place)
    row = iota((rows, 1), 0)
    late = row >= REQUEST_LENGTH
    offset = jnp.where(late, row - REQUEST_LENGTH, row)
    position = offset + jnp.where(late, c_a, 0)
    target = jnp.where(position < packed, position, position + d_a + d_b - first)
    target = jnp.where(offset < jnp.where(late, c_b, c_a), target, -1)
    out[...] = (iota((rows, rows), 1) == target).astype(F32).astype(BF16)


def seats(counts, place, rows, packed):
    return pl.pallas_call(
        functools.partial(seats_kernel, packed),
        grid_spec=pltpu.PrefetchScalarGridSpec(
            num_scalar_prefetch=2, grid=(1,), in_specs=[], out_specs=whole((rows, rows))
        ),
        out_shape=jax.ShapeDtypeStruct((rows, rows), BF16),
        compiler_params=params(),
        name="seats",
    )(counts, place)


def unpack_kernel(hot_ref, x_ref, spare_ref, out):
    packed = x_ref.shape[0]
    out[...] = (dot(hot_ref[:, :packed], x_ref[...]) + dot(hot_ref[:, packed:], spare_ref[...])).astype(BF16)


def unpack(hot, x, spare):
    shape = (hot.shape[0], x.shape[1])
    return pl.pallas_call(
        unpack_kernel,
        grid=(1,),
        in_specs=[whole(hot.shape), whole(x.shape), whole(spare.shape)],
        out_specs=whole(shape),
        out_shape=jax.ShapeDtypeStruct(shape, BF16),
        compiler_params=params(),
        name="unpack_rows",
    )(hot, x, spare)


def request_of(counts, place, slot, packed):
    c_a, c_b, d_a, _ = lengths(counts, place)
    n_mine, replica = c_a + c_b, place[0]
    own = slot < n_mine
    seat = jnp.where(own, slot, packed + slot - n_mine)
    mine = 2 * replica + (seat >= c_a).astype(I32)
    theirs = 2 * (1 - replica) + (seat >= d_a).astype(I32)
    return jnp.where(own, mine, theirs)


def fetch_kernel(held, adapter_of, location, place, *refs):
    count = (len(refs) - 1) // 2
    stores, outs = refs[:count], refs[count + 1 :]
    slot = location[adapter_of[pl.program_id(0)]] - place[0] * held
    mine = (slot >= 0) & (slot < held)
    for table, out in zip(stores, outs):
        block = table[0]
        out[...] = jnp.where(mine, block, jnp.zeros_like(block))


def fetch(stores, adapter_of, location, place, after):
    held, rank, width = stores[0].shape
    requests = adapter_of.shape[0]

    def at(i, adapter_of, location, place):
        slot = location[adapter_of[i]] - place[0] * held
        return jnp.clip(slot, 0, held - 1), 0, 0

    return pl.pallas_call(
        functools.partial(fetch_kernel, held),
        grid_spec=pltpu.PrefetchScalarGridSpec(
            num_scalar_prefetch=3,
            grid=(requests,),
            in_specs=[pl.BlockSpec((1, rank, width), at)] * len(stores)
            + [pl.BlockSpec(memory_space=pl.ANY)],
            out_specs=[pl.BlockSpec((rank, width), lambda i, *_: (i, 0))] * len(stores),
        ),
        out_shape=[jax.ShapeDtypeStruct((requests * rank, width), BF16)] * len(stores),
        compiler_params=params(LARGE),
        name="fetch_blocks",
    )(adapter_of, location, place, *stores, after)


def down_kernel(counts, place, x, v, own_q, own_o, other_q, other_o, out, blocks):
    rank = out.shape[1] // 2
    packed, width = x.shape
    requests = own_q.shape[0] // rank
    blocks[...] = jnp.zeros_like(blocks)
    who = request_of(counts, place, iota((packed, 1), 0), packed)
    total = jnp.zeros(out.shape, F32)
    for i in range(requests):
        rows = pl.ds(i * rank, rank)
        blocks[:rank, :width] = own_q[rows] + other_q[rows]
        blocks[rank:, width:] = own_o[rows] + other_o[rows]
        got = dot_t(x[...], blocks[:, :width]) + dot_t(v[...], blocks[:, width:])
        total = total + jnp.where(who == i, got, 0.0)
    out[...] = total


def down(counts, place, x, v, own, other):
    requests_rank, width = own[0].shape
    rank = requests_rank // 4
    packed = x.shape[0]
    half = (requests_rank, width)
    return pl.pallas_call(
        down_kernel,
        grid_spec=pltpu.PrefetchScalarGridSpec(
            num_scalar_prefetch=2,
            grid=(1,),
            in_specs=[whole(v.shape) for v in (x, v)] + [whole(half)] * 4,
            out_specs=whole((packed, 2 * rank)),
            scratch_shapes=[pltpu.VMEM((2 * rank, 2 * width), BF16)],
        ),
        out_shape=jax.ShapeDtypeStruct((packed, 2 * rank), F32),
        compiler_params=params(),
        name="down_rows",
    )(counts, place, x, v, *own, *other)


def up_kernel(counts, place, low, own_q, own_o, other_q, other_o, q_ref, o_ref, blocks):
    packed, both = low.shape
    rank = both // 2
    width = q_ref.shape[1]
    requests = own_q.shape[0] // rank
    blocks[...] = jnp.zeros_like(blocks)
    who = request_of(counts, place, iota((packed, 1), 0), packed)
    rows_low = low[...].astype(BF16).astype(F32)
    for i in range(requests):
        rows = pl.ds(i * rank, rank)
        blocks[pl.ds(2 * i * rank, rank), :width] = own_q[rows] + other_q[rows]
        blocks[pl.ds((2 * i + 1) * rank, rank), width:] = own_o[rows] + other_o[rows]
    wide = jnp.concatenate(
        [jnp.where(who == i, rows_low, 0.0).astype(BF16) for i in range(requests)], axis=1
    )
    q_ref[...] = adapter_scale * dot(wide, blocks[:, :width])
    o_ref[...] = adapter_scale * dot(wide, blocks[:, width:])


def up(counts, place, low, own, other):
    packed, both = low.shape
    requests_rank, width = own[0].shape
    half = (requests_rank, width)
    return pl.pallas_call(
        up_kernel,
        grid_spec=pltpu.PrefetchScalarGridSpec(
            num_scalar_prefetch=2,
            grid=(1,),
            in_specs=[whole(low.shape)]
            + [whole(half)] * 4,
            out_specs=[whole((packed, width))] * 2,
            scratch_shapes=[pltpu.VMEM((2 * requests_rank, 2 * width), BF16)],
        ),
        out_shape=[jax.ShapeDtypeStruct((packed, width), F32)] * 2,
        compiler_params=params(),
        name="up_rows",
    )(counts, place, low, *own, *other)


def shares_kernel(where, x_ref, w_ref, out):
    out[0] = dot(x_ref[...], w_ref[...])


def shares(where, start, count, x, weight):
    rows, width = x.shape
    return pl.pallas_call(
        shares_kernel,
        grid_spec=pltpu.PrefetchScalarGridSpec(
            num_scalar_prefetch=1,
            grid=(count,),
            in_specs=[
                whole(x.shape),
                pl.BlockSpec((width, width), lambda i, where: (0, where[start + i])),
            ],
            out_specs=pl.BlockSpec((1, rows, width), lambda i, where: (i, 0, 0)),
        ),
        out_shape=jax.ShapeDtypeStruct((count, rows, width), F32),
        compiler_params=params(LARGE),
        name="shares",
    )(where, x, weight)


def add_kernel(pieces, where, *refs):
    xs, ws, extra, out = refs[:pieces], refs[pieces : 2 * pieces], refs[2 * pieces : -1], refs[-1]
    total = dot(xs[0][...], ws[0][...])
    for x, w in zip(xs[1:], ws[1:]):
        total = total + dot(x[...], w[...])
    for more in extra:
        total = total + more[...]
    out[...] = total.astype(out.dtype)


def add_products(where, pieces, at, weight, addends, dtype=F32):
    rows, width = pieces[0].shape
    columns = weight.shape[1]
    step = columns // 2

    def rows_of(i):
        return pl.BlockSpec((width, step), lambda j, where: (where[at[i]], j))

    tall = pl.BlockSpec((rows, step), lambda j, where: (0, j))
    return pl.pallas_call(
        functools.partial(add_kernel, len(pieces)),
        grid_spec=pltpu.PrefetchScalarGridSpec(
            num_scalar_prefetch=1,
            grid=(2,),
            in_specs=[whole(p.shape) for p in pieces]
            + [rows_of(i) for i in range(len(pieces))]
            + [tall] * len(addends),
            out_specs=tall,
        ),
        out_shape=jax.ShapeDtypeStruct((rows, columns), dtype),
        compiler_params=params(LARGE),
        name="add_products",
    )(where, *pieces, *([weight] * len(pieces)), *addends)


def narrow(value):
    return (value * SUM_SCALE).astype(F16)


def widen(value):
    return value.astype(F32) * (1.0 / SUM_SCALE)


def tie(value, *others):
    return lax.optimization_barrier((value, others))[0]


def swap(total, bit, size):
    mine = (total * DOWN_SCALE).astype(F16)
    return send(mine, [(t, t ^ bit) for t in range(size)], f"down_sums_{bit}"), mine


def meet(moved, mine):
    return (mine.astype(F32) + moved.astype(F32)) * (1.0 / DOWN_SCALE)


def make(mesh):
    size = mesh.shape["tensor"]
    order = ring_order(size)
    steps = size // 2
    following = [(order[p], order[(p + 1) % size]) for p in range(size)]
    preceding = [(b, a) for a, b in following]
    offsets = [0] + [sign * d for d in range(1, steps) for sign in (1, -1)] + [steps]
    place_of = [order.index(t) for t in range(size)]

    def local(
        tokens, context, query_weight, output_weight,
        store_aq, store_bq, store_ao, store_bo,
        adapter_of, location, token_count,
    ):
        rows, width = tokens.shape
        packed = rows * 3 // 4
        spare = rows - packed
        half = packed // 2
        at = lax.axis_index("tensor")
        place = jnp.stack([lax.axis_index("replica")]).astype(I32)
        counts = token_count
        where = jnp.stack(
            [look_up(at, [order[(p + d) % size] for p in place_of]) for d in offsets]
        )

        tok = fill(counts, place, pack(counts, place, tokens), other_replica(tokens))
        ahead, behind = send(tok, following, "gather_up_1"), send(tok, preceding, "gather_down_1")
        ctx = fill(counts, tie(place, tok), pack(counts, tie(place, tok), context), other_replica(context))
        farthest = shares(where, size - 1, 1, ctx, output_weight)
        far = narrow(farthest[0])
        up_sum = send(far[:half], following, "scatter_up_1")
        down_sum = send(far[half:], preceding, "scatter_down_1")
        mine = fetch((store_aq, store_ao), adapter_of, location, place, tok)
        theirs = [other_replica(blocks) for blocks in mine]
        near = shares(tie(where, mine), size - 3, 2, ctx, output_weight)
        parts = down(counts, place, tok, tie(ctx, near), mine, theirs)
        bits = [1 << i for i in range(size.bit_length() - 1)]
        swapped = swap(parts, bits.pop(0), size)

        q, ready = None, parts
        for step in range(1, steps):
            got_up, got_down = lax.optimization_barrier((tie(ahead, ready), behind))
            if step < steps - 1:
                ahead = send(got_up, following, f"gather_up_{step + 1}")
                behind = send(got_down, preceding, f"gather_down_{step + 1}")
            else:
                up_half, down_half = lax.optimization_barrier((got_up[:half], got_down[half:]))
                ahead = send(up_half, following, f"gather_up_{step + 1}")
                behind = send(down_half, preceding, f"gather_down_{step + 1}")
                rest = tie(rest, up_half, down_half)
            if step == 1:
                rest = shares(where, 0, size - 3, tie(ctx, got_up, got_down), output_weight)
                pieces, at_pieces, sofar = [tok, got_down, got_up], [0, 1, 2], []
            else:
                pieces, at_pieces, sofar = [got_down, got_up], [2 * step - 1, 2 * step], [q]
            q = add_products(tie(where, rest), pieces, at_pieces, query_weight, sofar)
            if step == 2:
                mine = fetch((store_bq, store_bo), adapter_of, location, place, q)
            up_sum, down_sum, swapped = lax.optimization_barrier((tie(up_sum, q), down_sum, swapped))
            if swapped is not None:
                parts = meet(*swapped)
                swapped = None
            if bits:
                swapped = swap(tie(parts, up_sum), bits.pop(0), size)
            up_share, down_share = near[0], near[1]
            d = steps - step - 1
            near = rest[2 * d - 1], rest[2 * d]
            if step == 1:
                up_out = jnp.concatenate([up_share[:half] + widen(up_sum), up_share[half:]])
                down_out = jnp.concatenate([down_share[:half], down_share[half:] + widen(down_sum)])
            else:
                up_out, down_out = up_share + widen(up_sum), down_share + widen(down_sum)
            up_out, down_out = narrow(up_out), narrow(down_out)
            up_sum = send(up_out, following, f"scatter_up_{step + 1}")
            down_sum = send(down_out, preceding, f"scatter_down_{step + 1}")
            ready = (up_out, down_out)
        theirs = [other_replica(tie(blocks, up_out, down_out)) for blocks in mine]
        got_up, got_down, swapped = lax.optimization_barrier((tie(ahead, ready), behind, swapped))
        if swapped is not None:
            parts = meet(*swapped)
        for bit in bits:
            parts = meet(*swap(parts, bit, size))
        last = jnp.concatenate([got_up, got_down])
        up_q, up_o = up(counts, place, tie(parts, last), mine, theirs)
        q = add_products(where, [last], [size - 1], query_weight, [q, up_q], BF16)
        hot = seats(counts, tie(place, q), rows, packed)
        q_m = other_replica(q[packed - spare :])
        queries = unpack(hot, q, q_m)
        base = rest[0] + up_o
        up_sum, down_sum = lax.optimization_barrier((tie(up_sum, queries, base), down_sum))
        first = packed - spare
        o_last = (base[first:] + widen(up_sum[first:]) + widen(down_sum[first:])).astype(BF16)
        o_m = other_replica(o_last)
        o = (base + widen(up_sum) + widen(down_sum)).astype(BF16)
        attended = unpack(hot, o, o_m)
        return queries, attended

    return local


def solution(mesh):
    return jax.shard_map(
        make(mesh),
        mesh=mesh,
        in_specs=(
            P(("groups", "replica"), "tensor"),
            P(("groups", "replica"), "tensor"),
            P(None, "tensor"),
            P("tensor", None),
            P(("groups", "replica"), None, "tensor"),
            P(("groups", "replica"), None, "tensor"),
            P(("groups", "replica"), None, "tensor"),
            P(("groups", "replica"), None, "tensor"),
            P("groups"),
            P("groups"),
            P("groups"),
        ),
        out_specs=(P(("groups", "replica"), "tensor"), P(("groups", "replica"), "tensor")),
        check_vma=False,
    )
```

```python
import functools

import jax
import jax.numpy as jnp
from jax import lax
from jax.experimental import pallas as pl
from jax.experimental.pallas import tpu as pltpu
from jax.sharding import PartitionSpec as P

REQUEST_LENGTH = 256


adapter_scale = 0.5

SUM_SCALE = 8.0
DOWN_SCALE = 16.0

BF16 = jnp.bfloat16
F16 = jnp.float16
F32 = jnp.float32
I32 = jnp.int32

SMALL = 16 * 1024 * 1024
LARGE = 40 * 1024 * 1024
FULL = 62 * 1024 * 1024


def ring_order(size):
    if size == 8:
        return [0, 2, 4, 6, 7, 5, 3, 1]
    return list(range(size))


def send(value, pairs, name):
    with jax.named_scope(name):
        return lax.ppermute(value, "tensor", pairs)


def other_replica(value):
    return lax.ppermute(value, "replica", [(0, 1), (1, 0)])


def dot(a, b):
    return jnp.dot(a, b, preferred_element_type=F32)


def dot_t(a, b):
    return lax.dot_general(a, b, (((1,), (1,)), ((), ())), preferred_element_type=F32)


def look_up(index, table):
    out = I32(table[0])
    for i, entry in enumerate(table[1:], 1):
        out = jnp.where(index == i, I32(entry), out)
    return out


def whole(shape):
    return pl.BlockSpec(shape, lambda *_: (0,) * len(shape))


def params(limit=SMALL):
    return pltpu.CompilerParams(dimension_semantics=("arbitrary",), vmem_limit_bytes=limit)


def iota(shape, dim):
    return lax.broadcasted_iota(I32, shape, dim)


def lengths(counts, place):
    mine, theirs = 2 * place[0], 2 - 2 * place[0]
    return counts[mine], counts[mine + 1], counts[theirs], counts[theirs + 1]


def select_rows(home, x):
    hot = iota((home.shape[0], x.shape[0]), 1) == home
    return dot(hot.astype(F32).astype(BF16), x[...])


def home_of(position, live, c_a):
    home = jnp.where(position < c_a, position, REQUEST_LENGTH + position - c_a)
    return jnp.where(live, home, -1)


def pack_kernel(counts, place, x_ref, out):
    c_a, c_b, _, _ = lengths(counts, place)
    slot = iota((out.shape[0], 1), 0)
    out[...] = select_rows(home_of(slot, slot < c_a + c_b, c_a), x_ref).astype(BF16)


def pack(counts, place, x):
    rows, width = x.shape
    shape = (rows * 3 // 4, width)
    return pl.pallas_call(
        pack_kernel,
        grid_spec=pltpu.PrefetchScalarGridSpec(
            num_scalar_prefetch=2,
            grid=(1,),
            in_specs=[whole(x.shape)],
            out_specs=whole(shape),
        ),
        out_shape=jax.ShapeDtypeStruct(shape, BF16),
        compiler_params=params(LARGE),
        name="pack_rows",
    )(counts, place, x)


def fill_kernel(packed, counts, place, x_ref, theirs_ref, out):
    spare = out.shape[0]
    c_a, c_b, d_a, _ = lengths(counts, place)
    n_mine = c_a + c_b
    slot = iota((spare, 1), 0) + packed - spare
    home = packed + slot - n_mine - d_a + REQUEST_LENGTH - (2 * REQUEST_LENGTH - spare)
    there = select_rows(jnp.where(slot < n_mine, -1, home), theirs_ref)
    out[...] = (x_ref[...].astype(F32) + there).astype(BF16)


def fill(counts, place, x, theirs):
    packed, width = x.shape
    rows = theirs.shape[0]
    spare = rows - packed
    last = pl.BlockSpec((spare, width), lambda *_: (packed // spare - 1, 0))
    return pl.pallas_call(
        functools.partial(fill_kernel, packed),
        grid_spec=pltpu.PrefetchScalarGridSpec(
            num_scalar_prefetch=2,
            grid=(1,),
            in_specs=[last, pl.BlockSpec((spare, width), lambda *_: (rows // spare - 1, 0))],
            out_specs=last,
        ),
        out_shape=jax.ShapeDtypeStruct(x.shape, BF16),
        input_output_aliases={2: 0},
        compiler_params=params(LARGE),
        name="fill_rows",
    )(counts, place, x, theirs)


def seats_kernel(packed, counts, place, out):
    rows = out.shape[0]
    first = 2 * packed - rows
    c_a, c_b, d_a, d_b = lengths(counts, place)
    row = iota((rows, 1), 0)
    late = row >= REQUEST_LENGTH
    offset = jnp.where(late, row - REQUEST_LENGTH, row)
    position = offset + jnp.where(late, c_a, 0)
    target = jnp.where(position < packed, position, position + d_a + d_b - first)
    target = jnp.where(offset < jnp.where(late, c_b, c_a), target, -1)
    out[...] = (iota((rows, rows), 1) == target).astype(F32).astype(BF16)


def seats(counts, place, rows, packed):
    return pl.pallas_call(
        functools.partial(seats_kernel, packed),
        grid_spec=pltpu.PrefetchScalarGridSpec(
            num_scalar_prefetch=2, grid=(1,), in_specs=[], out_specs=whole((rows, rows))
        ),
        out_shape=jax.ShapeDtypeStruct((rows, rows), BF16),
        compiler_params=params(),
        name="seats",
    )(counts, place)


def unpack_kernel(hot_ref, x_ref, spare_ref, out):
    packed = x_ref.shape[0]
    out[...] = (dot(hot_ref[:, :packed], x_ref[...]) + dot(hot_ref[:, packed:], spare_ref[...])).astype(BF16)


def unpack(hot, x, spare):
    shape = (hot.shape[0], x.shape[1])
    return pl.pallas_call(
        unpack_kernel,
        grid=(1,),
        in_specs=[whole(hot.shape), whole(x.shape), whole(spare.shape)],
        out_specs=whole(shape),
        out_shape=jax.ShapeDtypeStruct(shape, BF16),
        compiler_params=params(),
        name="unpack_rows",
    )(hot, x, spare)


def unpack_first(hot, x):
    rows, (packed, width) = hot.shape[0], x.shape

    def kernel(hot_ref, x_ref, out):
        out[...] = dot(hot_ref[:, :packed], x_ref[...]).astype(BF16)

    return pl.pallas_call(
        kernel,
        grid=(1,),
        in_specs=[pl.BlockSpec((packed, rows), lambda j: (0, 0)), whole(x.shape)],
        out_specs=pl.BlockSpec((packed, width), lambda j: (0, 0)),
        out_shape=jax.ShapeDtypeStruct((rows, width), BF16),
        compiler_params=params(),
        name="unpack_first",
    )(hot, x)


def unpack_last(hot, x, spare, into):
    rows, (packed, width) = hot.shape[0], x.shape
    count = rows - packed
    last = pl.BlockSpec((count, width), lambda j: (packed // count, 0))

    def kernel(hot_ref, x_ref, spare_ref, into_ref, out):
        out[...] = (
            dot(hot_ref[:, :packed], x_ref[...]) + dot(hot_ref[:, packed:], spare_ref[...])
        ).astype(BF16)

    return pl.pallas_call(
        kernel,
        grid=(1,),
        in_specs=[
            pl.BlockSpec((count, rows), lambda j: (packed // count, 0)),
            whole(x.shape),
            whole(spare.shape),
            pl.BlockSpec(memory_space=pl.ANY),
        ],
        out_specs=last,
        out_shape=jax.ShapeDtypeStruct((rows, width), BF16),
        input_output_aliases={3: 0},
        compiler_params=params(),
        name="unpack_last",
    )(hot, x, spare, into)


def request_of(counts, place, slot, packed):
    c_a, c_b, d_a, _ = lengths(counts, place)
    n_mine, replica = c_a + c_b, place[0]
    own = slot < n_mine
    seat = jnp.where(own, slot, packed + slot - n_mine)
    mine = 2 * replica + (seat >= c_a).astype(I32)
    theirs = 2 * (1 - replica) + (seat >= d_a).astype(I32)
    return jnp.where(own, mine, theirs)


def fetch_kernel(held, adapter_of, location, place, *refs):
    count = (len(refs) - 1) // 2
    stores, outs = refs[:count], refs[count + 1 :]
    slot = location[adapter_of[pl.program_id(0)]] - place[0] * held
    mine = (slot >= 0) & (slot < held)
    for table, out in zip(stores, outs):
        block = table[0]
        out[...] = jnp.where(mine, block, jnp.zeros_like(block))


def fetch(stores, adapter_of, location, place, after):
    held, rank, width = stores[0].shape
    requests = adapter_of.shape[0]

    def at(i, adapter_of, location, place):
        slot = location[adapter_of[i]] - place[0] * held
        return jnp.clip(slot, 0, held - 1), 0, 0

    return pl.pallas_call(
        functools.partial(fetch_kernel, held),
        grid_spec=pltpu.PrefetchScalarGridSpec(
            num_scalar_prefetch=3,
            grid=(requests,),
            in_specs=[pl.BlockSpec((1, rank, width), at)] * len(stores)
            + [pl.BlockSpec(memory_space=pl.ANY)],
            out_specs=[pl.BlockSpec((rank, width), lambda i, *_: (i, 0))] * len(stores),
        ),
        out_shape=[jax.ShapeDtypeStruct((requests * rank, width), BF16)] * len(stores),
        compiler_params=params(LARGE),
        name="fetch_blocks",
    )(adapter_of, location, place, *stores, after)


def down_kernel(counts, place, x, v, own_q, own_o, other_q, other_o, out, blocks):
    rank = out.shape[1] // 2
    packed, width = x.shape
    requests = own_q.shape[0] // rank
    blocks[...] = jnp.zeros_like(blocks)
    who = request_of(counts, place, iota((packed, 1), 0), packed)
    total = jnp.zeros(out.shape, F32)
    for i in range(requests):
        rows = pl.ds(i * rank, rank)
        blocks[:rank, :width] = own_q[rows] + other_q[rows]
        blocks[rank:, width:] = own_o[rows] + other_o[rows]
        got = dot_t(x[...], blocks[:, :width]) + dot_t(v[...], blocks[:, width:])
        total = total + jnp.where(who == i, got, 0.0)
    out[...] = total


def down(counts, place, x, v, own, other):
    requests_rank, width = own[0].shape
    rank = requests_rank // 4
    packed = x.shape[0]
    half = (requests_rank, width)
    return pl.pallas_call(
        down_kernel,
        grid_spec=pltpu.PrefetchScalarGridSpec(
            num_scalar_prefetch=2,
            grid=(1,),
            in_specs=[whole(v.shape) for v in (x, v)] + [whole(half)] * 4,
            out_specs=whole((packed, 2 * rank)),
            scratch_shapes=[pltpu.VMEM((2 * rank, 2 * width), BF16)],
        ),
        out_shape=jax.ShapeDtypeStruct((packed, 2 * rank), F32),
        compiler_params=params(),
        name="down_rows",
    )(counts, place, x, v, *own, *other)


def up_kernel(counts, place, low, own_q, own_o, other_q, other_o, q_ref, o_ref, blocks):
    packed, both = low.shape
    rank = both // 2
    width = q_ref.shape[1]
    requests = own_q.shape[0] // rank
    blocks[...] = jnp.zeros_like(blocks)
    who = request_of(counts, place, iota((packed, 1), 0), packed)
    rows_low = low[...].astype(BF16).astype(F32)
    for i in range(requests):
        rows = pl.ds(i * rank, rank)
        blocks[pl.ds(2 * i * rank, rank), :width] = own_q[rows] + other_q[rows]
        blocks[pl.ds((2 * i + 1) * rank, rank), width:] = own_o[rows] + other_o[rows]
    wide = jnp.concatenate(
        [jnp.where(who == i, rows_low, 0.0).astype(BF16) for i in range(requests)], axis=1
    )
    q_ref[...] = adapter_scale * dot(wide, blocks[:, :width])
    o_ref[...] = adapter_scale * dot(wide, blocks[:, width:])


def up(counts, place, low, own, other):
    packed, both = low.shape
    requests_rank, width = own[0].shape
    half = (requests_rank, width)
    return pl.pallas_call(
        up_kernel,
        grid_spec=pltpu.PrefetchScalarGridSpec(
            num_scalar_prefetch=2,
            grid=(1,),
            in_specs=[whole(low.shape)]
            + [whole(half)] * 4,
            out_specs=[whole((packed, width))] * 2,
            scratch_shapes=[pltpu.VMEM((2 * requests_rank, 2 * width), BF16)],
        ),
        out_shape=[jax.ShapeDtypeStruct((packed, width), F32)] * 2,
        compiler_params=params(),
        name="up_rows",
    )(counts, place, low, *own, *other)


def shares_kernel(where, x_ref, w_ref, out):
    out[0] = dot(x_ref[...], w_ref[...])


def shares(where, start, count, x, weight):
    rows, width = x.shape
    return pl.pallas_call(
        shares_kernel,
        grid_spec=pltpu.PrefetchScalarGridSpec(
            num_scalar_prefetch=1,
            grid=(count,),
            in_specs=[
                whole(x.shape),
                pl.BlockSpec((width, width), lambda i, where: (0, where[start + i])),
            ],
            out_specs=pl.BlockSpec((1, rows, width), lambda i, where: (i, 0, 0)),
        ),
        out_shape=jax.ShapeDtypeStruct((count, rows, width), F32),
        compiler_params=params(LARGE),
        name="shares",
    )(where, x, weight)


def add_kernel(pieces, where, *refs):
    xs, ws, extra, out = refs[:pieces], refs[pieces : 2 * pieces], refs[2 * pieces : -1], refs[-1]
    total = dot(xs[0][...], ws[0][...])
    for x, w in zip(xs[1:], ws[1:]):
        total = total + dot(x[...], w[...])
    for more in extra:
        total = total + more[...]
    out[...] = total.astype(out.dtype)


def add_products(where, pieces, at, weight, addends, dtype=F32):
    rows, width = pieces[0].shape
    columns = weight.shape[1]
    step = columns // 2

    def rows_of(i):
        return pl.BlockSpec((width, step), lambda j, where: (where[at[i]], j))

    tall = pl.BlockSpec((rows, step), lambda j, where: (0, j))
    return pl.pallas_call(
        functools.partial(add_kernel, len(pieces)),
        grid_spec=pltpu.PrefetchScalarGridSpec(
            num_scalar_prefetch=1,
            grid=(2,),
            in_specs=[whole(p.shape) for p in pieces]
            + [rows_of(i) for i in range(len(pieces))]
            + [tall] * len(addends),
            out_specs=tall,
        ),
        out_shape=jax.ShapeDtypeStruct((rows, columns), dtype),
        compiler_params=params(LARGE),
        name="add_products",
    )(where, *pieces, *([weight] * len(pieces)), *addends)


def narrow(value):
    return (value * SUM_SCALE).astype(F16)


def widen(value):
    return value.astype(F32) * (1.0 / SUM_SCALE)


def tie(value, *others):
    return lax.optimization_barrier((value, others))[0]


def swap(total, bit, size):
    mine = (total * DOWN_SCALE).astype(F16)
    return send(mine, [(t, t ^ bit) for t in range(size)], f"down_sums_{bit}"), mine


def meet(moved, mine):
    return (mine.astype(F32) + moved.astype(F32)) * (1.0 / DOWN_SCALE)


def make(mesh):
    size = mesh.shape["tensor"]
    order = ring_order(size)
    steps = size // 2
    following = [(order[p], order[(p + 1) % size]) for p in range(size)]
    preceding = [(b, a) for a, b in following]
    offsets = [0] + [sign * d for d in range(1, steps) for sign in (1, -1)] + [steps]
    place_of = [order.index(t) for t in range(size)]

    def local(
        tokens, context, query_weight, output_weight,
        store_aq, store_bq, store_ao, store_bo,
        adapter_of, location, token_count,
    ):
        rows, width = tokens.shape
        packed = rows * 3 // 4
        spare = rows - packed
        half = packed // 2
        at = lax.axis_index("tensor")
        place = jnp.stack([lax.axis_index("replica")]).astype(I32)
        counts = token_count
        where = jnp.stack(
            [look_up(at, [order[(p + d) % size] for p in place_of]) for d in offsets]
        )

        tok = fill(counts, place, pack(counts, place, tokens), other_replica(tokens))
        ahead, behind = send(tok, following, "gather_up_1"), send(tok, preceding, "gather_down_1")
        ctx = fill(counts, tie(place, tok), pack(counts, tie(place, tok), context), other_replica(context))
        farthest = shares(where, size - 1, 1, ctx, output_weight)
        far = narrow(farthest[0])
        up_sum = send(far[:half], following, "scatter_up_1")
        down_sum = send(far[half:], preceding, "scatter_down_1")
        mine = fetch((store_aq, store_ao), adapter_of, location, place, tok)
        theirs = [other_replica(blocks) for blocks in mine]
        near = shares(tie(where, mine), size - 3, 2, ctx, output_weight)
        parts = down(counts, place, tok, tie(ctx, near), mine, theirs)
        bits = [1 << i for i in range(size.bit_length() - 1)]
        swapped = swap(parts, bits.pop(0), size)

        q, ready = None, parts
        for step in range(1, steps):
            got_up, got_down = lax.optimization_barrier((tie(ahead, ready), behind))
            if step < steps - 1:
                ahead = send(got_up, following, f"gather_up_{step + 1}")
                behind = send(got_down, preceding, f"gather_down_{step + 1}")
            else:
                up_half, down_half = lax.optimization_barrier((got_up[:half], got_down[half:]))
                ahead = send(up_half, following, f"gather_up_{step + 1}")
                behind = send(down_half, preceding, f"gather_down_{step + 1}")
                rest = tie(rest, up_half, down_half)
            if step == 1:
                rest = shares(where, 0, size - 3, tie(ctx, got_up, got_down), output_weight)
                pieces, at_pieces, sofar = [tok, got_down, got_up], [0, 1, 2], []
            else:
                pieces, at_pieces, sofar = [got_down, got_up], [2 * step - 1, 2 * step], [q]
            q = add_products(tie(where, rest), pieces, at_pieces, query_weight, sofar)
            if step == 2:
                mine = fetch((store_bq, store_bo), adapter_of, location, place, q)
            up_sum, down_sum, swapped = lax.optimization_barrier((tie(up_sum, q), down_sum, swapped))
            if swapped is not None:
                parts = meet(*swapped)
                swapped = None
            if bits:
                swapped = swap(tie(parts, up_sum), bits.pop(0), size)
            up_share, down_share = near[0], near[1]
            d = steps - step - 1
            near = rest[2 * d - 1], rest[2 * d]
            if step == 1:
                up_out = jnp.concatenate([up_share[:half] + widen(up_sum), up_share[half:]])
                down_out = jnp.concatenate([down_share[:half], down_share[half:] + widen(down_sum)])
            else:
                up_out, down_out = up_share + widen(up_sum), down_share + widen(down_sum)
            up_out, down_out = narrow(up_out), narrow(down_out)
            up_sum = send(up_out, following, f"scatter_up_{step + 1}")
            down_sum = send(down_out, preceding, f"scatter_down_{step + 1}")
            ready = (up_out, down_out)
        theirs = [other_replica(tie(blocks, up_out, down_out)) for blocks in mine]
        got_up, got_down, swapped = lax.optimization_barrier((tie(ahead, ready), behind, swapped))
        if swapped is not None:
            parts = meet(*swapped)
        for bit in bits:
            parts = meet(*swap(parts, bit, size))
        last = jnp.concatenate([got_up, got_down])
        up_q, up_o = up(counts, place, tie(parts, last), mine, theirs)
        q = add_products(where, [last], [size - 1], query_weight, [q, up_q], BF16)
        hot = seats(counts, tie(place, q), rows, packed)
        q_m = other_replica(q[packed - spare :])
        queries = unpack(hot, q, q_m)
        base = rest[0] + up_o
        up_sum, down_sum = lax.optimization_barrier((tie(up_sum, queries, base), down_sum))
        first = packed - spare
        o_last = (base[first:] + widen(up_sum[first:]) + widen(down_sum[first:])).astype(BF16)
        o_m = other_replica(o_last)
        o = (base + widen(up_sum) + widen(down_sum)).astype(BF16)
        attended = unpack_first(hot, o)
        attended = unpack_last(hot, o, tie(o_m, attended), attended)
        return queries, attended

    return local


def solution(mesh):
    return jax.shard_map(
        make(mesh),
        mesh=mesh,
        in_specs=(
            P(("groups", "replica"), "tensor"),
            P(("groups", "replica"), "tensor"),
            P(None, "tensor"),
            P("tensor", None),
            P(("groups", "replica"), None, "tensor"),
            P(("groups", "replica"), None, "tensor"),
            P(("groups", "replica"), None, "tensor"),
            P(("groups", "replica"), None, "tensor"),
            P("groups"),
            P("groups"),
            P("groups"),
        ),
        out_specs=(P(("groups", "replica"), "tensor"), P(("groups", "replica"), "tensor")),
        check_vma=False,
    )
```
